32 devices in a mesh: parts: 2 (over y), win: 16 (over z, x, core).
Axes of the slice: x: 2, y: 2, z: 4, core: 2. Of those that a mesh axis runs over, the one named last changes fastest.
Arguments:
- records: bfloat16 [2048, 8192], P('win', 'parts'), parts along dimension 1, may hold values from -45 to 45
- templates: bfloat16 [2, 64, 128, 512], P(None, None, 'win'), may hold values from -16 to 16
- panel_start: int32 [4], P('parts'), parts along dimension 0, may hold values from 0 to 1920
Outputs:
- traces: float32 [8192, 128], P(('parts', 'win')), parts along dimension 0
The draws below stay inside these ranges and needn't reach their ends.
There are 2 independent parts, one for each index of `parts`. The reference program is written for one: setup_inputs(seed, part) draws one part's arguments, and reference() takes and returns one part's arrays. A program takes and returns all parts, laid end to end along the dimension named above; an argument that names none is the same for every part. Nothing has to cross between parts.
Inputs may be any that keep to these rules, and one draw needn't show every extreme that they name: Each panel covers channels panel_start to panel_start + 127; panels may share channels.
All inputs are finite; a program needn't handle non-finite values.
Results may differ from the reference program's by a relative error of at most 0.0003.
Values may be sent and summed in bfloat16 or wider, within the bound.
No kernel may reach another device: no remote copies, remote signals or barrier semaphores. Data moves between devices by JAX's collectives and lax.ppermute only.
A program may use at most 128 MiB of HBM per device.

```python
import math
import jax
import jax.numpy as jnp
from jax import lax

CHANNELS = 2048
P_SIZE = 2
G = 64
CT = 128
L = 512
S_DEV = 256
SAMPLES = 4096
N_WIN = 16


def draw_records(key, part):
    key = jax.random.fold_in(key, 11)
    first, second, third = jax.random.split(key, 3)
    noise = jnp.clip(jax.random.normal(first, (CHANNELS, SAMPLES), jnp.float32), -5.0, 5.0)
    low, high = (math.log(0.3), math.log(3.0))
    channel_scale = jnp.exp(jax.random.uniform(second, (CHANNELS, 1), jnp.float32, low, high))
    levels = jnp.exp(jax.random.uniform(third, (16,), jnp.float32, -1.0, 1.0))
    envelope = levels[jnp.arange(SAMPLES) * 16 // SAMPLES]
    return (noise * channel_scale * envelope[None, :]).astype(jnp.bfloat16)


def draw_templates(key, part):
    key = jax.random.fold_in(key, 23)
    first, second = jax.random.split(key)
    position = jnp.arange(CT, dtype=jnp.float32) / (CT - 1)
    values = jnp.clip(jax.random.normal(first, (P_SIZE, G, CT, L), jnp.float32), -4.0, 4.0)
    taper = jnp.sqrt(1.0 + 2.0 * position)
    gains = jnp.exp(jax.random.uniform(second, (P_SIZE, G, 1, 1), jnp.float32, math.log(0.5), math.log(2.0)))
    return (values * gains * taper[None, None, :, None]).astype(jnp.bfloat16)


def setup_inputs(seed: int = 0, part: int = 0) -> dict:
    streams_of = jax.random.split(jax.random.key(seed), 4)
    part_keys = jax.random.split(jax.random.fold_in(streams_of[3], part), 4)
    records = draw_records(jax.random.fold_in(jax.random.fold_in(streams_of[3], part), 71), part)
    templates = draw_templates(jax.random.fold_in(streams_of[3], 71), part)
    panel_start = jax.random.randint(part_keys[2], (P_SIZE,), 0, CHANNELS - CT + 1).astype(jnp.int32)
    return {"records": records, "templates": templates, "panel_start": panel_start}


epsilon = 1e-06

def unfold(strip, width, number):
    leading = strip.shape[:-1]
    length = strip.shape[-1]
    tiled = jnp.tile(strip, (1,) * len(leading) + (width + 1,))
    cut = tiled[..., :width * (length + 1)].reshape(leading + (width, length + 1))
    return cut[..., :number]

def reference(records, templates, panel_start):
    padded = jnp.pad(records, ((0, 0), (0, L - 1)))
    chosen = jnp.stack([lax.dynamic_slice_in_dim(padded, panel_start[panel], CT, 0) for panel in range(P_SIZE)])
    squares = lax.optimization_barrier(jnp.sum(jnp.square(chosen.astype(jnp.float32)), axis=1))
    energy = lax.reduce_window(squares, jnp.float32(0.0), lax.add, (1, L), (1, 1), 'VALID')
    template_norm = lax.optimization_barrier(jnp.sum(jnp.square(templates.astype(jnp.float32)), axis=(2, 3)))
    flattened = templates.reshape(P_SIZE, G, CT * L)

    def segment(block_id):
        strip = lax.dynamic_slice_in_dim(chosen, (block_id * S_DEV).astype(jnp.int32), S_DEV + L - 1, 2)
        unfolded = unfold(strip, L, S_DEV)
        return jnp.stack([jnp.dot(flattened[panel], unfolded[panel].reshape(CT * L, S_DEV), preferred_element_type=jnp.float32) for panel in range(P_SIZE)])
    blocks = lax.map(segment, jnp.arange(N_WIN, dtype=jnp.int32))
    correlation = jnp.transpose(blocks, (0, 3, 1, 2)).reshape(SAMPLES, P_SIZE, G)
    scaled = math.sqrt(CT * L) * correlation * lax.rsqrt(template_norm)[None, :, :]
    traces = scaled * lax.rsqrt(energy + epsilon).T[:, :, None]
    return traces.reshape(SAMPLES, P_SIZE * G)
```

```python
import math

import jax
import jax.numpy as jnp
from jax import lax
from jax.experimental import pallas as pl
from jax.experimental.pallas import tpu as pltpu
from jax.sharding import PartitionSpec as P

CT = 128
L = 512
LANES = 128
epsilon = 1e-06
f32 = jnp.float32
bf16 = jnp.bfloat16
VMEM_BYTES = 60 * 2**20


def iota(shape, dim):
    return lax.broadcasted_iota(jnp.int32, shape, dim)


def dot(a, b, dims=(((1,), (0,)), ((), ()))):
    return lax.dot_general(a, b, dims, preferred_element_type=f32)


def split3(v):
    high = v.astype(bf16)
    rest = v - high.astype(f32)
    middle = rest.astype(bf16)
    return high, middle, (rest - middle.astype(f32)).astype(bf16)


def pick(v, m):
    return sum(dot(part, m) for part in split3(v))


def picked(m, v):
    return sum(dot(m, part) for part in split3(v))


def shift_kernel(own_ref, other_ref, w_ref, norm_ref, rows_ref, *, phases):
    gc = own_ref.shape[0]
    groups = LANES // 2
    each = gc // groups
    channels = 2 * each
    pad = channels * phases
    total = rows_ref.shape[0]
    rows_ref[pl.ds(0, pad), :] = jnp.zeros((pad, LANES), f32)
    rows_ref[pl.ds(pad + L * channels, total - pad - L * channels), :] = jnp.zeros(
        (total - pad - L * channels, LANES), f32
    )
    norm = jnp.zeros((1, LANES), f32)
    row, lane = iota((gc, LANES), 0), iota((gc, LANES), 1)
    for side, ref in enumerate((own_ref, other_ref)):
        for c in range(each):
            choose = (row == (lane % groups) * each + c).astype(f32).astype(bf16)
            piece = dot(ref[...], choose, (((0,), (0,)), ((), ())))
            norm = norm + jnp.sum(piece * piece, axis=0, keepdims=True)
            rows_ref[pl.ds(pad + side * each + c, L, stride=channels), :] = piece
    norm_ref[...] = jnp.broadcast_to(norm, norm_ref.shape)
    low = iota((256, LANES), 1) < groups
    for q in range(w_ref.shape[0]):
        for tile in range(phases // 2):
            start = pad + 256 * q - 2 * tile * channels
            even = rows_ref[pl.ds(start, 256), :]
            odd = rows_ref[pl.ds(start - channels, 256), :]
            w_ref[q, :, tile * LANES : (tile + 1) * LANES] = jnp.where(low, even, odd).astype(bf16)


def shifted(own, other, phases, pairs):
    channels = 2 * own.shape[1]
    rows = 256 * pairs + channels * phases
    gc = own.shape[0] * own.shape[1]
    return pl.pallas_call(
        lambda *refs: shift_kernel(*refs, phases=phases),
        out_shape=(
            jax.ShapeDtypeStruct((pairs, 256, phases * 64), bf16),
            jax.ShapeDtypeStruct((8, LANES), f32),
        ),
        scratch_shapes=[pltpu.VMEM((rows, LANES), f32)],
        compiler_params=pltpu.CompilerParams(vmem_limit_bytes=VMEM_BYTES),
        cost_estimate=pl.CostEstimate(flops=2**30, bytes_accessed=2**24, transcendentals=0),
        name="shift_templates",
    )(own.reshape(gc, L), other.reshape(gc, L))


def correlate_kernel(*refs, phases, za, zb, n_early, n_late):
    ix_ref = refs[0]
    early = refs[1 : 1 + n_early]
    late = refs[1 + n_early : 1 + n_early + n_late]
    w_ref, norm_ref = refs[1 + n_early + n_late : 3 + n_early + n_late]
    zs = n_early
    outs = refs[3 + n_early + n_late :]
    keep_a, send_a, keep_b = outs[:3]
    send_b = outs[3 : 2 + zs]
    spread_ref, rows_ref, slide_ref, acc_ref, wbuf_ref, sem = outs[2 + zs :]

    pairs = w_ref.shape[0]
    for q in range(pairs):
        pltpu.make_async_copy(w_ref.at[q], wbuf_ref.at[q], sem.at[q]).start()

    channels = LANES // phases
    first, second = sum(r[...] for r in early[1:]) + early[0][...], late[0][...] + late[1][...]
    repeat = (iota((channels, LANES), 0) == iota((channels, LANES), 1) % channels).astype(f32).astype(bf16)
    ta, tb = first.shape[1], second.shape[1]
    spread_ref[pl.ds(0, ta), :] = dot(first, repeat, (((0,), (0,)), ((), ())))
    spread_ref[pl.ds(ta, tb), :] = dot(second, repeat, (((0,), (0,)), ((), ())))
    count = (ta + tb) // phases
    phase = iota((count, LANES), 1) // channels
    rows = jnp.zeros((count, LANES), f32)
    for k in range(phases):
        rows = jnp.where(phase == k, spread_ref[pl.ds(k, count, stride=phases), :], rows)
    total = rows_ref.shape[0]
    rows_ref[pl.ds(0, count), :] = rows
    rows_ref[pl.ds(count, total - count), :] = jnp.zeros((total - count, LANES), f32)

    span = slide_ref.shape[1]
    for k in range(min(8, pairs)):
        slide_ref[k, :, 0:LANES] = rows_ref[pl.ds(2 * k, span), :].astype(bf16)
        slide_ref[k, :, LANES:] = rows_ref[pl.ds(2 * k + 1, span), :].astype(bf16)

    per = L // phases
    left, right = iota((LANES, LANES), 0) // channels, iota((LANES, LANES), 1) % (2 * phases)
    inside = right < phases
    tail = (inside & (left >= right)).astype(f32).astype(bf16)
    head = (inside & (left < right)).astype(f32).astype(bf16)
    squares = rows * rows
    sums = jnp.broadcast_to(jnp.sum(squares, axis=1, keepdims=True), squares.shape)
    distance = iota((count, count), 1) - iota((count, count), 0)
    band = ((distance >= 1) & (distance < per)).astype(f32).astype(bf16)
    begin = pick(squares, head)
    begin = jnp.concatenate([begin[per:], jnp.zeros((per, LANES), f32)], axis=0)
    energy = pick(squares, tail) + picked(band, sums) + begin

    for q in range(pairs):
        pltpu.make_async_copy(w_ref.at[q], wbuf_ref.at[q], sem.at[q]).wait()
        window = slide_ref[q % 8, pl.ds(16 * (q // 8), count), :]
        term = dot(window, wbuf_ref[q])
        if q == 0:
            acc_ref[...] = term
        else:
            acc_ref[...] += term

    groups = LANES // 2
    sub = per // 8
    place = iota((LANES, LANES), 1)
    wanted = (place // (2 * phases)) * phases + place % (2 * phases) - phases
    scatter = ((place % (2 * phases) >= phases) & (iota((LANES, LANES), 0) == wanted)).astype(f32).astype(bf16)
    norm = pick(norm_ref[...], scatter)
    rows_ref[pl.ds(0, count), :] = energy
    lane_group = iota((8, LANES), 1) // (2 * phases)
    x, z = ix_ref[0], ix_ref[1]
    tiles = phases // 2

    def extras(chip):
        at = pl.multiple_of(chip * per, 8)
        e = jnp.zeros((8, LANES), f32)
        for k in range(sub):
            e = jnp.where(lane_group == k, rows_ref[pl.ds(at + 8 * k, 8), :], e)
        valid = iota((8, LANES), 1) % (2 * phases) < phases
        return jnp.where(valid, e, norm)

    def write(ref, slot, chip, lo, hi):
        at = pl.multiple_of(chip * per, 8)
        for tile in range(tiles):
            a, b = max(lo, tile * per), min(hi, (tile + 1) * per)
            if a < b:
                ref[slot, a - lo : b - lo, :] = acc_ref[
                    pl.ds(pl.multiple_of(at + a - tile * per, 8), b - a), tile * LANES : (tile + 1) * LANES
                ]
        if hi > 256:
            ref[slot, 256 - lo : 264 - lo, :] = extras(chip)

    for k in range(zs):
        zk = jnp.bitwise_xor(z, k)
        write(send_a, k, zk * 2 + 1 - x, 0, za)
        write(keep_a, k, zk * 2 + x, 0, za)
        ref = keep_b if k == 0 else send_b[k - 1]
        write(ref, 0, zk * 2 + x, za, za + zb)
        write(ref, 1, zk * 2 + 1 - x, za, za + zb)


def correlate(ix, early, late, w, norm, za, zb):
    zs = len(early)
    phases = w.shape[2] // 64
    t = early[0].shape[1] + late[0].shape[1]
    count = t // phases
    pairs = w.shape[0]
    span = count + 16 * ((pairs - 1) // 8)
    vmem = pl.BlockSpec(memory_space=pltpu.VMEM)
    return pl.pallas_call(
        lambda *refs: correlate_kernel(
            *refs, phases=phases, za=za, zb=zb, n_early=len(early), n_late=len(late)
        ),
        out_shape=tuple(
            [jax.ShapeDtypeStruct((zs, za, LANES), f32)] * 2 + [jax.ShapeDtypeStruct((2, zb, LANES), f32)] * zs
        ),
        in_specs=[pl.BlockSpec(memory_space=pltpu.SMEM)]
        + [vmem] * (len(early) + len(late))
        + [pl.BlockSpec(memory_space=pl.ANY), vmem],
        out_specs=tuple([vmem] * (2 + zs)),
        scratch_shapes=[
            pltpu.VMEM((t, LANES), f32),
            pltpu.VMEM((span + 16, LANES), f32),
            pltpu.VMEM((min(8, pairs), span, 256), bf16),
            pltpu.VMEM((count, w.shape[2]), f32),
            pltpu.VMEM(w.shape, bf16),
            pltpu.SemaphoreType.DMA((pairs,)),
        ],
        compiler_params=pltpu.CompilerParams(vmem_limit_bytes=VMEM_BYTES),
        cost_estimate=pl.CostEstimate(flops=2**33, bytes_accessed=2**24, transcendentals=0),
        name="correlate",
    )(ix, *early, *late, w, norm)


def scale_kernel(*refs, phases, na, nb):
    ix_ref = refs[0]
    a = sum(r[0] for r in refs[1 : 1 + na])
    b = sum(r[0] for r in refs[1 + na : 1 + na + nb])
    mine_ref, other_ref = refs[1 + na + nb :]
    groups = LANES // 2
    per = L // phases
    sub = per // 8
    block = jnp.concatenate([a, b], axis=0)
    extra = block[256:264]
    place = iota((LANES, LANES), 0)
    wanted = (place // (2 * phases)) * phases + place % (2 * phases) - phases
    gather = (
        ((place % (2 * phases) >= phases) & (iota((LANES, LANES), 1) % groups == wanted)).astype(f32).astype(bf16)
    )
    norm = math.sqrt(CT * L) * lax.rsqrt(pick(extra, gather))
    energy = lax.rsqrt(extra + epsilon)
    low = iota((8, LANES), 1) < groups
    first = ix_ref[2] == 0
    half = per // 2
    for tile in range(phases // 2):
        parts = []
        for k in range(sub):
            at = 2 * phases * k + 2 * tile
            scale = jnp.where(low, energy[:, at : at + 1], energy[:, at + 1 : at + 2]) * norm
            parts.append(block[tile * per + 8 * k : tile * per + 8 * k + 8] * scale)
        whole = jnp.concatenate(parts, axis=0) if sub > 1 else parts[0]
        lower, upper = whole[:half], whole[half:]
        mine_ref[tile] = jnp.where(first, lower, upper)
        other_ref[tile] = jnp.where(first, upper, lower)


def scaled(ix, a, b, phases):
    vmem = pl.BlockSpec(memory_space=pltpu.VMEM)
    half = jax.ShapeDtypeStruct((phases // 2, L // phases // 2, LANES), f32)
    return pl.pallas_call(
        lambda *refs: scale_kernel(*refs, phases=phases, na=len(a), nb=len(b)),
        out_shape=(half, half),
        in_specs=[pl.BlockSpec(memory_space=pltpu.SMEM)] + [vmem] * (len(a) + len(b)),
        out_specs=(vmem, vmem),
        cost_estimate=pl.CostEstimate(flops=2**18, bytes_accessed=2**20, transcendentals=0),
        name="scale",
    )(ix, *a, *b)


def weave_kernel(ix_ref, mine_ref, got_ref, out_ref):
    tiles, half, _ = mine_ref.shape
    low = iota((half, LANES), 1) < LANES // 2
    first = ix_ref[2] == 0
    for tile in range(tiles):
        mine, got = mine_ref[tile], got_ref[tile]
        zero, one = jnp.where(first, mine, got), jnp.where(first, got, mine)
        out_ref[pl.ds(2 * tile, half, stride=2 * tiles), :] = jnp.where(low, zero, pltpu.roll(one, LANES // 2, 1))
        out_ref[pl.ds(2 * tile + 1, half, stride=2 * tiles), :] = jnp.where(low, pltpu.roll(zero, LANES // 2, 1), one)


def weave(ix, mine, got):
    vmem = pl.BlockSpec(memory_space=pltpu.VMEM)
    tiles, half, _ = mine.shape
    return pl.pallas_call(
        weave_kernel,
        out_shape=jax.ShapeDtypeStruct((2 * tiles * half, LANES), f32),
        in_specs=[pl.BlockSpec(memory_space=pltpu.SMEM), vmem, vmem],
        out_specs=vmem,
        cost_estimate=pl.CostEstimate(flops=2**16, bytes_accessed=2**18, transcendentals=0),
        name="weave",
    )(ix, mine, got)


def local(records, templates, panel_start):
    devices = lax.axis_size("win")
    me = lax.axis_index("win")
    chips = devices // 2
    zs = chips // 2
    core, chip = me % 2, me // 2
    x, z = chip % 2, chip // 2
    ix = jnp.stack([x, z, core]).astype(jnp.int32)
    held, t = records.shape
    own = CT // devices
    per_chip = 2 * own
    phases = LANES // per_chip
    pairs = (L // phases + 2) // 2

    def swap(value, bit):
        return lax.ppermute(value, "win", [(d, d ^ bit) for d in range(devices)])

    kx = jnp.arange(2)[:, None, None]
    kz = jnp.arange(zs)[None, :, None]
    k = jnp.arange(per_chip)[None, None, :]

    def routed(panel):
        target = jnp.bitwise_xor(z, kz) * 2 + jnp.bitwise_xor(x, kx)
        channel = target * per_chip + (k + own * panel) % per_chip
        row = (panel_start[panel] + channel - me * held).reshape(CT, 1)
        return (row == jnp.arange(held)[None, :]).astype(bf16)

    away = jnp.dot(routed(1 - core), records, preferred_element_type=f32).astype(bf16)
    home = jnp.dot(routed(core), records, preferred_element_type=f32).astype(bf16)
    home = home + swap(away, 1)
    wanted = lax.dynamic_index_in_dim(templates, core, 0, keepdims=False)
    given = lax.dynamic_index_in_dim(templates, 1 - core, 0, keepdims=False)
    w, norm = shifted(wanted, swap(given, 1), phases, pairs)

    ta = t * 5 // 8 // LANES * LANES
    home = home.reshape(2, zs, per_chip, t)
    a, b = home[..., :ta], home[..., ta:]
    a = a[0] + swap(a[1], 2)
    b = b[:, 0] + sum(swap(b[:, i], 4 * i) for i in range(1, zs))
    early = [a[0]] + [swap(a[i], 4 * i) for i in range(1, zs)]
    late = [b[0], swap(b[1], 2)]

    za, zb = 168, 96
    keep_a, send_a, keep_b, *send_b = correlate(ix, early, late, w, norm, za, zb)
    a = keep_a + swap(send_a, 2)
    b = keep_b + sum(swap(v, 4 * (i + 1)) for i, v in enumerate(send_b))
    a = [a[0:1]] + [swap(a[i : i + 1], 4 * i) for i in range(1, zs)]
    b = [b[0:1], swap(b[1:2], 2)]
    mine, other = scaled(ix, a, b, phases)
    return weave(ix, mine, swap(other, 1))


def solution(mesh):
    placed = (P("win", "parts"), P(None, None, "win", None), P("parts"))
    return jax.shard_map(
        local, mesh=mesh, in_specs=placed, out_specs=P(("parts", "win"), None), check_vma=False
    )
```

```python
import math

import jax
import jax.numpy as jnp
from jax import lax
from jax.experimental import pallas as pl
from jax.experimental.pallas import tpu as pltpu
from jax.sharding import PartitionSpec as P

CT = 128
L = 512
LANES = 128
epsilon = 1e-06
f32 = jnp.float32
bf16 = jnp.bfloat16
SPARE = 12 * 2**20
IN_VMEM = pl.BlockSpec(memory_space=pltpu.VMEM)
SMALL = pltpu.CompilerParams(vmem_limit_bytes=8 * 2**20)


def iota(shape, dim):
    return lax.broadcasted_iota(jnp.int32, shape, dim)


def dot(a, b, dims=(((1,), (0,)), ((), ()))):
    return lax.dot_general(a, b, dims, preferred_element_type=f32)


def split3(v):
    high = v.astype(bf16)
    rest = v - high.astype(f32)
    middle = rest.astype(bf16)
    return high, middle, (rest - middle.astype(f32)).astype(bf16)


def pick(v, m):
    return sum(dot(part, m) for part in split3(v))


def picked(m, v):
    return sum(dot(m, part) for part in split3(v))


def shift_kernel(own_ref, other_ref, w_ref, norm_ref, rows_ref, *, phases):
    gc = own_ref.shape[0]
    groups = LANES // 2
    each = gc // groups
    channels = 2 * each
    versions, total, _ = w_ref.shape
    pad = channels * phases
    front = rows_ref.shape[0] - total
    rows_ref[pl.ds(0, front + pad), :] = jnp.zeros((front + pad, LANES), f32)
    rows_ref[pl.ds(front + pad + L * channels, total - pad - L * channels), :] = jnp.zeros(
        (total - pad - L * channels, LANES), f32
    )
    norm = jnp.zeros((1, LANES), f32)
    width = min(2, each) * LANES
    row, lane = iota((gc, width), 0), iota((gc, width), 1)
    for side, ref in enumerate((own_ref, other_ref)):
        for c in range(0, each, width // LANES):
            choose = (row == (lane % groups) * each + c + lane // LANES).astype(f32).astype(bf16)
            piece = dot(ref[...], choose, (((0,), (0,)), ((), ())))
            for i in range(width // LANES):
                one = piece[:, i * LANES : (i + 1) * LANES]
                norm = norm + jnp.sum(one * one, axis=0, keepdims=True)
                rows_ref[pl.ds(front + pad + side * each + c + i, L, stride=channels), :] = one
    norm_ref[...] = jnp.broadcast_to(norm, norm_ref.shape)
    low = iota((256, LANES), 1) < groups
    for v in range(versions):
        for at in range(0, total, 256):
            size = min(256, total - at)
            start = front + at - 2 * channels * v
            even = rows_ref[pl.ds(start, size), :]
            odd = rows_ref[pl.ds(start - channels, size), :]
            w_ref[v, at : at + size, :] = jnp.where(low[:size], even, odd).astype(bf16)


def shifted(own, other, phases, pairs):
    channels = 2 * own.shape[1]
    versions = max(1, 8 // channels)
    total = 256 * pairs + channels * phases
    front = (2 * versions - 1) * channels + 8
    front = (front + 7) // 8 * 8
    gc = own.shape[0] * own.shape[1]
    return pl.pallas_call(
        lambda *refs: shift_kernel(*refs, phases=phases),
        out_shape=(
            jax.ShapeDtypeStruct((versions, total, LANES), bf16),
            jax.ShapeDtypeStruct((8, LANES), f32),
        ),
        scratch_shapes=[pltpu.VMEM((front + total, LANES), f32)],
        compiler_params=pltpu.CompilerParams(vmem_limit_bytes=512 * (front + total) + SPARE),
        cost_estimate=pl.CostEstimate(flops=2**30, bytes_accessed=2**24, transcendentals=0),
        name="shift_templates",
    )(own.reshape(gc, L), other.reshape(gc, L))


def bits_of(devices):
    x, z, *rest = [1 << i for i in range(1, devices.bit_length() - 1)]
    return [x, z] + rest, [z, x] + rest


def panel_of(device, devices):
    return sum(device >> i & 1 for i in range(devices.bit_length() - 1)) % 2


def target_of(slot, panel, devices):
    mine, theirs = bits_of(devices)
    chip = jnp.zeros_like(slot)
    for i, (p, q) in enumerate(zip(mine, theirs)):
        chip += (slot >> (len(mine) - 1 - i) & 1) * jnp.where(panel == 0, p, q)
    return chip // 2


def spread(pieces, spread_ref, phases):
    value = sum(r[...] for r in pieces[1:]) + pieces[0][...]
    channels, t = value.shape
    repeat = (iota((channels, LANES), 0) == iota((channels, LANES), 1) % channels).astype(f32).astype(bf16)
    spread_ref[...] = dot(value, repeat, (((0,), (0,)), ((), ())))
    count = t // phases
    phase = iota((count, LANES), 1) // channels
    rows = jnp.zeros((count, LANES), f32)
    for k in range(phases):
        rows = jnp.where(phase == k, spread_ref[pl.ds(k, count, stride=phases), :], rows)
    return rows


def fill_slide(rows_ref, slide_ref):
    span = slide_ref.shape[1]
    for k in range(slide_ref.shape[0]):
        slide_ref[k, :, 0:LANES] = rows_ref[pl.ds(2 * k, span), :].astype(bf16)
        slide_ref[k, :, LANES:] = rows_ref[pl.ds(2 * k + 1, span), :].astype(bf16)


def energies(squares, m, phases):
    n = squares.shape[0]
    channels = LANES // phases
    per = L // phases
    left, right = iota((LANES, LANES), 0) // channels, iota((LANES, LANES), 1) % (2 * phases)
    inside = right < phases
    tail = (inside & (left >= right)).astype(f32).astype(bf16)
    head = (inside & (left < right)).astype(f32).astype(bf16)
    sums = jnp.broadcast_to(jnp.sum(squares, axis=1, keepdims=True), squares.shape)
    distance = iota((m, n), 1) - iota((m, n), 0)
    band = ((distance >= 1) & (distance < per)).astype(f32).astype(bf16)
    begin = pick(squares[per : min(n, per + m)], head)
    if per + m > n:
        begin = jnp.concatenate([begin, jnp.zeros((per + m - n, LANES), f32)], axis=0)
    return pick(squares[:m], tail) + picked(band, sums) + begin


def correlate_tiles(slide_ref, w_ref, acc_ref, m, tiles, phases):
    versions = w_ref.shape[0]
    channels = LANES // phases
    pairs = (w_ref.shape[1] - LANES) // 256

    def shifts(q, tile):
        v = tile % versions
        return w_ref[v, pl.ds(LANES + 256 * q - 2 * channels * (tile - v), 256), :]

    for q in range(pairs):
        window = slide_ref[q % 8, pl.ds(16 * (q // 8), m), :]
        term = dot(window, jnp.concatenate([shifts(q, tile) for tile in tiles], axis=1))
        if q == 0:
            acc_ref[pl.ds(0, m), :] = term
        else:
            acc_ref[pl.ds(0, m), :] += term


def late_kernel(*refs, phases):
    *pieces, w_ref, out_rows, out_energy, out_acc, spread_ref, rows_ref, slide_ref = refs
    rows = spread(pieces, spread_ref, phases)
    count = rows.shape[0]
    out_rows[...] = rows
    rows_ref[pl.ds(0, count), :] = rows
    rows_ref[pl.ds(count, rows_ref.shape[0] - count), :] = jnp.zeros((rows_ref.shape[0] - count, LANES), f32)
    fill_slide(rows_ref, slide_ref)
    out_energy[...] = energies(rows * rows, count, phases)
    correlate_tiles(slide_ref, w_ref, out_acc, count, range(phases // 2), phases)


def write_blocks(send_ref, keep_ref, acc_ref, lead, per, devices):
    me = lax.axis_index("win")
    kept = keep_ref.shape[0]
    for slot in range(2 * kept):
        chip = jnp.bitwise_xor(me // 2, target_of(jnp.int32(slot), panel_of(me, devices), devices))
        at = pl.multiple_of(chip * per, 8)
        ref = keep_ref if slot < kept else send_ref
        for tile in range(acc_ref.shape[1] // LANES):
            ref[slot % kept, tile * per : (tile + 1) * per, :] = acc_ref[
                pl.ds(at, per), tile * LANES : (tile + 1) * LANES
            ]
        if lead is not None:
            ref[slot % kept, LANES:, :] = lead(at)


def early_kernel(*refs, phases, devices):
    *pieces, w_ref, rest_rows, rest_acc, send_ref, keep_ref, rows_ref, slide_ref, spread_ref, acc_ref = refs
    rows = spread(pieces, spread_ref, phases)
    m = rows.shape[0]
    n = m + rest_rows.shape[0]
    rows_ref[pl.ds(0, m), :] = rows
    rows_ref[pl.ds(m, n - m), :] = rest_rows[...]
    fill_slide(rows_ref, slide_ref)
    acc_ref[pl.ds(m, n - m), :] = rest_acc[:, : acc_ref.shape[1]]
    correlate_tiles(slide_ref, w_ref, acc_ref, m, range(phases // 4), phases)
    write_blocks(send_ref, keep_ref, acc_ref, None, L // phases, devices)


def middle_kernel(rows_ref, slide_ref, w_ref, norm_ref, rest_energy, rest_acc, send_ref, keep_ref, energy_ref, acc_ref, *, phases, devices):
    n = rows_ref.shape[0]
    m = n - rest_energy.shape[0]
    squares = rows_ref[...]
    energy_ref[pl.ds(0, m), :] = energies(squares * squares, m, phases)
    energy_ref[pl.ds(m, n - m), :] = rest_energy[...]
    acc_ref[pl.ds(m, n - m), :] = rest_acc[:, acc_ref.shape[1] :]
    correlate_tiles(slide_ref, w_ref, acc_ref, m, range(phases // 4, phases // 2), phases)

    per = L // phases
    place = iota((LANES, LANES), 1)
    wanted = (place // (2 * phases)) * phases + place % (2 * phases) - phases
    scatter = ((place % (2 * phases) >= phases) & (iota((LANES, LANES), 0) == wanted)).astype(f32).astype(bf16)
    norm = pick(norm_ref[...], scatter)
    lane = iota((8, LANES), 1)

    def extras(at):
        e = norm
        for k in range(per // 8):
            e = jnp.where(
                (lane // (2 * phases) == k) & (lane % (2 * phases) < phases), energy_ref[pl.ds(at + 8 * k, 8), :], e
            )
        return e

    write_blocks(send_ref, keep_ref, acc_ref, extras, per, devices)


def grant(shapes):
    return pltpu.CompilerParams(vmem_limit_bytes=sum(math.prod(s.shape) * 4 for s in shapes) + SPARE)


def slide_shape(m, phases):
    pairs = (L // phases + 2) // 2
    return (min(8, pairs), m + 16 * ((pairs - 1) // 8), 256)


def correlate_late(pieces, w, phases):
    t = pieces[0].shape[1]
    count = t // phases
    slide = slide_shape(count, phases)
    shapes = [
        pltpu.VMEM((t, LANES), f32),
        pltpu.VMEM((slide[1] + 16, LANES), f32),
        pltpu.VMEM(slide, bf16),
    ]
    return pl.pallas_call(
        lambda *refs: late_kernel(*refs, phases=phases),
        out_shape=(
            jax.ShapeDtypeStruct((count, LANES), f32),
            jax.ShapeDtypeStruct((count, LANES), f32),
            jax.ShapeDtypeStruct((count, phases * 64), f32),
        ),
        in_specs=[IN_VMEM] * (len(pieces) + 1),
        out_specs=(IN_VMEM, IN_VMEM, IN_VMEM),
        scratch_shapes=shapes,
        compiler_params=grant(shapes),
        cost_estimate=pl.CostEstimate(flops=2**31, bytes_accessed=2**22, transcendentals=0),
        name="correlate_late",
    )(*pieces, w)


def correlate_early(pieces, w, rest_rows, rest_acc, phases, devices):
    t = pieces[0].shape[1]
    m = t // phases
    n = m + rest_rows.shape[0]
    kept = devices // 4
    shapes = [pltpu.VMEM((t, LANES), f32), pltpu.VMEM((n, phases * 32), f32)]
    block = jax.ShapeDtypeStruct((kept, LANES, LANES), f32)
    return pl.pallas_call(
        lambda *refs: early_kernel(*refs, phases=phases, devices=devices),
        out_shape=(
            block,
            block,
            jax.ShapeDtypeStruct((n, LANES), f32),
            jax.ShapeDtypeStruct(slide_shape(m, phases), bf16),
        ),
        in_specs=[IN_VMEM] * (len(pieces) + 3),
        out_specs=(IN_VMEM,) * 4,
        scratch_shapes=shapes,
        compiler_params=grant(shapes),
        cost_estimate=pl.CostEstimate(flops=2**32, bytes_accessed=2**24, transcendentals=0),
        name="correlate_early",
    )(*pieces, w, rest_rows, rest_acc)


def correlate_middle(rows, slide, w, norm, rest_energy, rest_acc, phases, devices):
    n = rows.shape[0]
    kept = devices // 4
    shapes = [pltpu.VMEM((n, LANES), f32), pltpu.VMEM((n, phases * 32), f32)]
    block = jax.ShapeDtypeStruct((kept, LANES + 8, LANES), f32)
    return pl.pallas_call(
        lambda *refs: middle_kernel(*refs, phases=phases, devices=devices),
        out_shape=(block, block),
        in_specs=[IN_VMEM] * 6,
        out_specs=(IN_VMEM, IN_VMEM),
        scratch_shapes=shapes,
        compiler_params=grant(shapes),
        cost_estimate=pl.CostEstimate(flops=2**33, bytes_accessed=2**24, transcendentals=0),
        name="correlate_middle",
    )(rows, slide, w, norm, rest_energy, rest_acc)


def halves_kernel(*refs, phases, na, nb):
    mine_ref, other_ref = refs[na + nb :]
    a = sum(r[0] for r in refs[:na])
    b = sum(r[0] for r in refs[na : na + nb])
    block = jnp.concatenate([a, b], axis=0)
    per = L // phases
    half = per // 2
    first = lax.axis_index("win") % 2 == 0
    for tile in range(phases // 2):
        lower = block[tile * per : tile * per + half]
        upper = block[tile * per + half : (tile + 1) * per]
        mine_ref[tile * half : (tile + 1) * half] = jnp.where(first, lower, upper)
        other_ref[tile * half : (tile + 1) * half] = jnp.where(first, upper, lower)
    mine_ref[128:136] = block[256:264]
    other_ref[128:136] = block[256:264]


def halves(a, b, phases):
    half = jax.ShapeDtypeStruct((136, LANES), f32)
    return pl.pallas_call(
        lambda *refs: halves_kernel(*refs, phases=phases, na=len(a), nb=len(b)),
        out_shape=(half, half),
        in_specs=[IN_VMEM] * (len(a) + len(b)),
        out_specs=(IN_VMEM, IN_VMEM),
        compiler_params=SMALL,
        cost_estimate=pl.CostEstimate(flops=2**18, bytes_accessed=2**20, transcendentals=0),
        name="halves",
    )(*a, *b)


def finish_kernel(mine_ref, got_ref, out_ref, *, phases, devices):
    groups = LANES // 2
    per = L // phases
    half = per // 2
    me = lax.axis_index("win")
    first = me % 2 == 0
    straight = panel_of(me, devices) == 0
    place = iota((LANES, LANES), 0)
    wanted = (place // (2 * phases)) * phases + place % (2 * phases) - phases
    gather = (
        ((place % (2 * phases) >= phases) & (iota((LANES, LANES), 1) % groups == wanted)).astype(f32).astype(bf16)
    )
    low = iota((half, LANES), 1) < groups
    sides = []
    for ref in (mine_ref, got_ref):
        extra = ref[128:136]
        norm = math.sqrt(CT * L) * lax.rsqrt(pick(extra, gather))[:1]
        scale = lax.rsqrt(extra + epsilon)
        sides.append((ref, norm, scale))
    for tile in range(phases // 2):
        scaled = []
        for ref, norm, scale in sides:
            columns = []
            for phase in (2 * tile, 2 * tile + 1):
                if half >= 8:
                    count = half // 8
                    at = [2 * phases * k + phase for k in range(2 * count)]
                    pieces = [scale[:, i : i + 1] for i in at]
                    columns.append(
                        jnp.concatenate(
                            [jnp.where(first, pieces[k], pieces[k + count]) for k in range(count)], axis=0
                        )
                    )
                else:
                    columns.append(
                        jnp.where(first, scale[:half, phase : phase + 1], scale[half : 2 * half, phase : phase + 1])
                    )
            rows = ref[tile * half : (tile + 1) * half]
            scaled.append(rows * (jnp.where(low, columns[0], columns[1]) * norm))
        mine, got = scaled
        zero, one = jnp.where(straight, mine, got), jnp.where(straight, got, mine)
        out_ref[pl.ds(2 * tile, half, stride=phases), :] = jnp.where(low, zero, pltpu.roll(one, groups, 1))
        out_ref[pl.ds(2 * tile + 1, half, stride=phases), :] = jnp.where(low, pltpu.roll(zero, groups, 1), one)


def finish(mine, got, phases, devices):
    return pl.pallas_call(
        lambda *refs: finish_kernel(*refs, phases=phases, devices=devices),
        out_shape=jax.ShapeDtypeStruct((L // 2, LANES), f32),
        in_specs=[IN_VMEM, IN_VMEM],
        out_specs=IN_VMEM,
        compiler_params=SMALL,
        cost_estimate=pl.CostEstimate(flops=2**18, bytes_accessed=2**18, transcendentals=0),
        name="finish",
    )(mine, got)


def route_kernel(start_ref, records_ref, early_ref, late_ref, *, for_sibling, devices):
    me = lax.axis_index("win")
    panel = panel_of(me, devices)
    if for_sibling:
        panel = 1 - panel
    held = records_ref.shape[0]
    per_chip = 2 * CT // devices
    row = iota((CT, held), 0)
    target = jnp.bitwise_xor(target_of(row // per_chip, panel, devices), me // 2)
    core = jnp.bitwise_xor(panel, panel_of(2 * target, devices))
    channel = target * per_chip + (row % per_chip + per_chip // 2 * core) % per_chip
    routed = (channel + start_ref[panel] - me * held == iota((CT, held), 1)).astype(f32).astype(bf16)
    half = early_ref.shape[1]
    late_ref[...] = dot(routed, records_ref[:, half:]).astype(bf16)
    early_ref[...] = dot(routed, records_ref[:, :half]).astype(bf16)


def route(panel_start, records, for_sibling, devices):
    half = jax.ShapeDtypeStruct((CT, records.shape[1] // 2), bf16)
    return pl.pallas_call(
        lambda *refs: route_kernel(*refs, for_sibling=for_sibling, devices=devices),
        out_shape=(half, half),
        in_specs=[pl.BlockSpec(memory_space=pltpu.SMEM), IN_VMEM],
        out_specs=(IN_VMEM, IN_VMEM),
        compiler_params=pltpu.CompilerParams(vmem_limit_bytes=SPARE),
        cost_estimate=pl.CostEstimate(flops=2**27, bytes_accessed=2**21, transcendentals=0),
        name="route_away" if for_sibling else "route_home",
    )(panel_start, records)


def add_kernel(kept_ref, got_ref, keep_ref, send_ref):
    half = keep_ref.shape[0]
    keep_ref[...] = kept_ref[:half] + got_ref[:half]
    send_ref[...] = kept_ref[half:] + got_ref[half:]


def sum_kernel(kept_ref, got_ref, sum_ref):
    sum_ref[...] = kept_ref[...] + got_ref[...]


def summed(kept, got):
    return pl.pallas_call(
        sum_kernel,
        out_shape=jax.ShapeDtypeStruct(kept.shape, kept.dtype),
        in_specs=[IN_VMEM, IN_VMEM],
        out_specs=IN_VMEM,
        compiler_params=SMALL,
        cost_estimate=pl.CostEstimate(flops=2**33, bytes_accessed=2**20, transcendentals=0),
        name="sum",
    )(kept, got)


def added(kept, got):
    half = kept.shape[0] // 2
    if kept.dtype == bf16 and half % 16:
        whole = kept + got
        return whole[:half], whole[half:]
    part = jax.ShapeDtypeStruct((half, *kept.shape[1:]), kept.dtype)
    return pl.pallas_call(
        add_kernel,
        out_shape=(part, part),
        in_specs=[IN_VMEM, IN_VMEM],
        out_specs=(IN_VMEM, IN_VMEM),
        compiler_params=SMALL,
        cost_estimate=pl.CostEstimate(flops=2**32, bytes_accessed=2**20, transcendentals=0),
        name="add",
    )(kept, got)


def local(records, templates, panel_start):
    devices = lax.axis_size("win")
    panel = panel_of(lax.axis_index("win"), devices)
    phases = devices // 2
    pairs = (L // phases + 2) // 2
    orders = bits_of(devices)

    def sibling(value):
        return lax.ppermute(value, "win", [(d, d ^ 1) for d in range(devices)])

    def exchange(value, step):
        return lax.ppermute(value, "win", [(d, d ^ 1 ^ orders[panel_of(d, devices)][step]) for d in range(devices)])

    def scattered(keep, send, step):
        got = exchange(send, step)
        if step == len(orders[0]) - 1:
            return keep, got
        return scattered(*added(keep, got), step + 1)

    away_early, away_late = route(panel_start, records, True, devices)
    got_late, got_early = sibling(away_late), sibling(away_early)
    home_early, home_late = route(panel_start, records, False, devices)
    wanted = lax.dynamic_index_in_dim(templates, panel, 0, keepdims=False)
    given = lax.dynamic_index_in_dim(templates, 1 - panel, 0, keepdims=False)
    w, norm = shifted(wanted, sibling(given), phases, pairs)

    late = scattered(*added(home_late, got_late), 0)
    early = scattered(*added(home_early, got_early), 0)
    rest_rows, rest_energy, rest_acc = correlate_late(late, w, phases)
    send_a, keep_a, rows, slide = correlate_early(early, w, rest_rows, rest_acc, phases, devices)
    send_b, keep_b = correlate_middle(rows, slide, w, norm, rest_energy, rest_acc, phases, devices)
    a = scattered(keep_a, send_a, 0)
    b = scattered(keep_b, send_b, 0)
    mine, other = halves([summed(*a)], b, phases)
    return finish(mine, sibling(other), phases, devices)


def solution(mesh):
    placed = (P("win", "parts"), P(None, None, "win", None), P("parts"))
    return jax.shard_map(
        local, mesh=mesh, in_specs=placed, out_specs=P(("parts", "win"), None), check_vma=False
    )
```

```python
import math

import jax
import jax.numpy as jnp
from jax import lax
from jax.experimental import pallas as pl
from jax.experimental.pallas import tpu as pltpu
from jax.sharding import PartitionSpec as P

CT = 128
L = 512
LANES = 128
epsilon = 1e-06
f32 = jnp.float32
bf16 = jnp.bfloat16
SPARE = 12 * 2**20
IN_VMEM = pl.BlockSpec(memory_space=pltpu.VMEM)
SMALL = pltpu.CompilerParams(vmem_limit_bytes=8 * 2**20)


def iota(shape, dim):
    return lax.broadcasted_iota(jnp.int32, shape, dim)


def dot(a, b, dims=(((1,), (0,)), ((), ()))):
    return lax.dot_general(a, b, dims, preferred_element_type=f32)


def split3(v):
    high = v.astype(bf16)
    rest = v - high.astype(f32)
    middle = rest.astype(bf16)
    return high, middle, (rest - middle.astype(f32)).astype(bf16)


def pick(v, m):
    return sum(dot(part, m) for part in split3(v))


def picked(m, v):
    return sum(dot(m, part) for part in split3(v))


def shift_kernel(templates_ref, other_ref, w_ref, norm_ref, rows_ref, *, phases, devices):
    gc = other_ref.shape[0]
    panel = panel_of(lax.axis_index("win"), devices)
    groups = LANES // 2
    each = gc // groups
    channels = 2 * each
    versions, total, _ = w_ref.shape
    pad = channels * phases
    front = rows_ref.shape[0] - total
    rows_ref[pl.ds(0, front + pad), :] = jnp.zeros((front + pad, LANES), f32)
    rows_ref[pl.ds(front + pad + L * channels, total - pad - L * channels), :] = jnp.zeros(
        (total - pad - L * channels, LANES), f32
    )
    norm = jnp.zeros((1, LANES), f32)
    width = min(2, each) * LANES
    row, lane = iota((gc, width), 0), iota((gc, width), 1)
    for side, ref in enumerate((templates_ref.at[panel], other_ref)):
        for c in range(0, each, width // LANES):
            choose = (row == (lane % groups) * each + c + lane // LANES).astype(f32).astype(bf16)
            piece = dot(ref[...], choose, (((0,), (0,)), ((), ())))
            for i in range(width // LANES):
                one = piece[:, i * LANES : (i + 1) * LANES]
                norm = norm + jnp.sum(one * one, axis=0, keepdims=True)
                rows_ref[pl.ds(front + pad + side * each + c + i, L, stride=channels), :] = one
    norm_ref[...] = jnp.broadcast_to(norm, norm_ref.shape)
    low = iota((256, LANES), 1) < groups
    for v in range(versions):
        for at in range(0, total, 256):
            size = min(256, total - at)
            start = front + at - 2 * channels * v
            even = rows_ref[pl.ds(start, size), :]
            odd = rows_ref[pl.ds(start - channels, size), :]
            w_ref[v, at : at + size, :] = jnp.where(low[:size], even, odd).astype(bf16)


def shifted(templates, other, phases, pairs):
    channels = 2 * other.shape[1]
    versions = max(1, 8 // channels)
    total = 256 * pairs + channels * phases
    front = (2 * versions - 1) * channels + 8
    front = (front + 7) // 8 * 8
    gc = other.shape[0] * other.shape[1]
    return pl.pallas_call(
        lambda *refs: shift_kernel(*refs, phases=phases, devices=2 * phases),
        out_shape=(
            jax.ShapeDtypeStruct((versions, total, LANES), bf16),
            jax.ShapeDtypeStruct((8, LANES), f32),
        ),
        scratch_shapes=[pltpu.VMEM((front + total, LANES), f32)],
        compiler_params=pltpu.CompilerParams(vmem_limit_bytes=512 * (front + total) + SPARE),
        cost_estimate=pl.CostEstimate(flops=2**30, bytes_accessed=2**24, transcendentals=0),
        name="shift_templates",
    )(templates.reshape(-1, gc, L), other.reshape(gc, L))


def bits_of(devices):
    x, z, *rest = [1 << i for i in range(1, devices.bit_length() - 1)]
    return [x, z] + rest, [z, x] + rest


def panel_of(device, devices):
    return sum(device >> i & 1 for i in range(devices.bit_length() - 1)) % 2


def target_of(slot, panel, devices):
    mine, theirs = bits_of(devices)
    chip = jnp.zeros_like(slot)
    for i, (p, q) in enumerate(zip(mine, theirs)):
        chip += (slot >> (len(mine) - 1 - i) & 1) * jnp.where(panel == 0, p, q)
    return chip // 2


def spread(pieces, spread_ref, phases):
    value = sum(r[...] for r in pieces[1:]) + pieces[0][...]
    channels, t = value.shape
    repeat = (iota((channels, LANES), 0) == iota((channels, LANES), 1) % channels).astype(f32).astype(bf16)
    spread_ref[...] = dot(value, repeat, (((0,), (0,)), ((), ())))
    count = t // phases
    phase = iota((count, LANES), 1) // channels
    rows = jnp.zeros((count, LANES), f32)
    for k in range(phases):
        rows = jnp.where(phase == k, spread_ref[pl.ds(k, count, stride=phases), :], rows)
    return rows


def fill_slide(rows_ref, slide_ref):
    span = slide_ref.shape[1]
    for k in range(slide_ref.shape[0]):
        slide_ref[k, :, 0:LANES] = rows_ref[pl.ds(2 * k, span), :].astype(bf16)
        slide_ref[k, :, LANES:] = rows_ref[pl.ds(2 * k + 1, span), :].astype(bf16)


def energies(squares, m, phases):
    n = squares.shape[0]
    channels = LANES // phases
    per = L // phases
    left, right = iota((LANES, LANES), 0) // channels, iota((LANES, LANES), 1) % (2 * phases)
    inside = right < phases
    tail = (inside & (left >= right)).astype(f32).astype(bf16)
    head = (inside & (left < right)).astype(f32).astype(bf16)
    sums = jnp.broadcast_to(jnp.sum(squares, axis=1, keepdims=True), squares.shape)
    distance = iota((m, n), 1) - iota((m, n), 0)
    band = ((distance >= 1) & (distance < per)).astype(f32).astype(bf16)
    begin = pick(squares[per : min(n, per + m)], head)
    if per + m > n:
        begin = jnp.concatenate([begin, jnp.zeros((per + m - n, LANES), f32)], axis=0)
    return pick(squares[:m], tail) + picked(band, sums) + begin


def correlate_tiles(slides, w_ref, acc_ref, tiles, phases):
    versions = w_ref.shape[0]
    channels = LANES // phases
    pairs = (w_ref.shape[1] - LANES) // 256
    m = sum(count for _, count in slides)

    def shifts(q, tile):
        v = tile % versions
        return w_ref[v, pl.ds(LANES + 256 * q - 2 * channels * (tile - v), 256), :]

    for q in range(pairs):
        window = [slide[q % 8, pl.ds(16 * (q // 8), count), :] for slide, count in slides]
        window = window[0] if len(window) == 1 else jnp.concatenate(window, axis=0)
        term = dot(window, jnp.concatenate([shifts(q, tile) for tile in tiles], axis=1))
        if q == 0:
            acc_ref[pl.ds(0, m), :] = term
        else:
            acc_ref[pl.ds(0, m), :] += term


def late_kernel(*refs, phases):
    *pieces, w_ref, out_rows, out_energy, out_slide, out_acc, spread_ref, rows_ref = refs
    rows = spread(pieces, spread_ref, phases)
    count = rows.shape[0]
    out_rows[...] = rows
    rows_ref[pl.ds(0, count), :] = rows
    rows_ref[pl.ds(count, rows_ref.shape[0] - count), :] = jnp.zeros((rows_ref.shape[0] - count, LANES), f32)
    fill_slide(rows_ref, out_slide)
    out_energy[...] = energies(rows * rows, count, phases)
    correlate_tiles([(out_slide, count)], w_ref, out_acc, range(phases // 4), phases)


def write_blocks(send_ref, keep_ref, acc_ref, lead, per, devices):
    me = lax.axis_index("win")
    kept = keep_ref.shape[0]
    for slot in range(2 * kept):
        chip = jnp.bitwise_xor(me // 2, target_of(jnp.int32(slot), panel_of(me, devices), devices))
        at = pl.multiple_of(chip * per, 8)
        ref = keep_ref if slot < kept else send_ref
        for tile in range(acc_ref.shape[1] // LANES):
            ref[slot % kept, tile * per : (tile + 1) * per, :] = acc_ref[
                pl.ds(at, per), tile * LANES : (tile + 1) * LANES
            ]
        if lead is not None:
            ref[slot % kept, LANES:, :] = lead(at)


def early_kernel(*refs, phases, devices):
    *pieces, w_ref, norm_ref, rest_rows, rest_energy, rest_acc = refs[: len(refs) - 7]
    send_ref, keep_ref, slide_ref, rows_ref, spread_ref, energy_ref, acc_ref = refs[len(refs) - 7 :]
    rows = spread(pieces, spread_ref, phases)
    m = rows.shape[0]
    n = m + rest_rows.shape[0]
    rows_ref[pl.ds(0, m), :] = rows
    rows_ref[pl.ds(m, n - m), :] = rest_rows[...]
    fill_slide(rows_ref, slide_ref)
    acc_ref[pl.ds(m, n - m), :] = rest_acc[...]
    correlate_tiles([(slide_ref, m)], w_ref, acc_ref, range(phases // 4), phases)

    squares = rows_ref[...]
    energy_ref[pl.ds(0, m), :] = energies(squares * squares, m, phases)
    energy_ref[pl.ds(m, n - m), :] = rest_energy[...]
    per = L // phases
    place = iota((LANES, LANES), 1)
    wanted = (place // (2 * phases)) * phases + place % (2 * phases) - phases
    scatter = ((place % (2 * phases) >= phases) & (iota((LANES, LANES), 0) == wanted)).astype(f32).astype(bf16)
    norm = pick(norm_ref[...], scatter)
    lane = iota((8, LANES), 1)

    def extras(at):
        e = norm
        for k in range(per // 8):
            e = jnp.where(
                (lane // (2 * phases) == k) & (lane % (2 * phases) < phases), energy_ref[pl.ds(at + 8 * k, 8), :], e
            )
        return e

    write_blocks(send_ref, keep_ref, acc_ref, extras, per, devices)


def rest_kernel(early_slide, late_slide, w_ref, send_ref, keep_ref, acc_ref, *, rows, phases, devices):
    slides = list(zip((early_slide, late_slide), rows))
    correlate_tiles(slides, w_ref, acc_ref, range(phases // 4, phases // 2), phases)
    write_blocks(send_ref, keep_ref, acc_ref, None, L // phases, devices)


def grant(shapes):
    return pltpu.CompilerParams(vmem_limit_bytes=sum(math.prod(s.shape) * 4 for s in shapes) + SPARE)


def slide_shape(m, phases):
    pairs = (L // phases + 2) // 2
    return (min(8, pairs), m + 16 * ((pairs - 1) // 8), 256)


def correlate_late(pieces, w, phases):
    t = pieces[0].shape[1]
    count = t // phases
    slide = slide_shape(count, phases)
    shapes = [pltpu.VMEM((t, LANES), f32), pltpu.VMEM((slide[1] + 16, LANES), f32)]
    return pl.pallas_call(
        lambda *refs: late_kernel(*refs, phases=phases),
        out_shape=(
            jax.ShapeDtypeStruct((count, LANES), f32),
            jax.ShapeDtypeStruct((count, LANES), f32),
            jax.ShapeDtypeStruct(slide, bf16),
            jax.ShapeDtypeStruct((count, phases * 32), f32),
        ),
        in_specs=[IN_VMEM] * (len(pieces) + 1),
        out_specs=(IN_VMEM,) * 4,
        scratch_shapes=shapes,
        compiler_params=grant(shapes),
        cost_estimate=pl.CostEstimate(flops=2**31, bytes_accessed=2**22, transcendentals=0),
        name="correlate_late",
    )(*pieces, w)


def correlate_early(pieces, w, norm, rest, phases, devices):
    t = pieces[0].shape[1]
    m = t // phases
    n = m + rest[0].shape[0]
    shapes = [
        pltpu.VMEM((n, LANES), f32),
        pltpu.VMEM((t, LANES), f32),
        pltpu.VMEM((n, LANES), f32),
        pltpu.VMEM((n, phases * 32), f32),
    ]
    block = jax.ShapeDtypeStruct((devices // 4, LANES + 8, LANES), f32)
    return pl.pallas_call(
        lambda *refs: early_kernel(*refs, phases=phases, devices=devices),
        out_shape=(block, block, jax.ShapeDtypeStruct(slide_shape(m, phases), bf16)),
        in_specs=[IN_VMEM] * (len(pieces) + 5),
        out_specs=(IN_VMEM,) * 3,
        scratch_shapes=shapes,
        compiler_params=grant(shapes),
        cost_estimate=pl.CostEstimate(flops=2**32, bytes_accessed=2**24, transcendentals=0),
        name="correlate_early",
    )(*pieces, w, norm, *rest)


def correlate_rest(early_slide, late_slide, w, rows, phases, devices):
    shapes = [pltpu.VMEM((sum(rows), phases * 32), f32)]
    block = jax.ShapeDtypeStruct((devices // 4, LANES, LANES), f32)
    return pl.pallas_call(
        lambda *refs: rest_kernel(*refs, rows=rows, phases=phases, devices=devices),
        out_shape=(block, block),
        in_specs=[IN_VMEM] * 3,
        out_specs=(IN_VMEM, IN_VMEM),
        scratch_shapes=shapes,
        compiler_params=grant(shapes),
        cost_estimate=pl.CostEstimate(flops=2**33, bytes_accessed=2**24, transcendentals=0),
        name="correlate_rest",
    )(early_slide, late_slide, w)


def cut(block, phases):
    per = L // phases
    half = per // 2
    starts = range(0, LANES, per)
    return (
        jnp.concatenate([block[at : at + half] for at in starts], axis=0),
        jnp.concatenate([block[at + half : at + per] for at in starts], axis=0),
    )


def halves_kernel(kept_ref, got_ref, mine_ref, other_ref, *, phases):
    first = lax.axis_index("win") % 2 == 0
    block = kept_ref[0] + got_ref[0]
    lower, upper = cut(block, phases)
    rows = LANES // 2
    mine_ref[0:rows] = jnp.where(first, lower, upper)
    other_ref[0:rows] = jnp.where(first, upper, lower)
    if block.shape[0] > LANES:
        mine_ref[rows:] = block[LANES:]
        other_ref[rows:] = block[LANES:]


def halves(kept, got, phases):
    half = jax.ShapeDtypeStruct((kept.shape[1] - LANES // 2, LANES), f32)
    return pl.pallas_call(
        lambda *refs: halves_kernel(*refs, phases=phases),
        out_shape=(half, half),
        in_specs=[IN_VMEM, IN_VMEM],
        out_specs=(IN_VMEM, IN_VMEM),
        compiler_params=SMALL,
        cost_estimate=pl.CostEstimate(flops=2**32, bytes_accessed=2**20, transcendentals=0),
        name="halves",
    )(kept, got)


def woven(straight, mine, got):
    groups = LANES // 2
    low = iota(mine.shape, 1) < groups
    zero, one = jnp.where(straight, mine, got), jnp.where(straight, got, mine)
    return jnp.where(low, zero, pltpu.roll(one, groups, 1)), jnp.where(low, pltpu.roll(zero, groups, 1), one)


def scale_kernel(mine_ref, got_ref, even_ref, odd_ref, mine_scale, got_scale, *, phases, devices):
    groups = LANES // 2
    per = L // phases
    half = per // 2
    tiles = phases // 4
    me = lax.axis_index("win")
    first = me % 2 == 0
    straight = panel_of(me, devices) == 0
    place = iota((LANES, LANES), 0)
    wanted = (place // (2 * phases)) * phases + place % (2 * phases) - phases
    gather = (
        ((place % (2 * phases) >= phases) & (iota((LANES, LANES), 1) % groups == wanted)).astype(f32).astype(bf16)
    )
    low = iota((half, LANES), 1) < groups
    sides = []
    for ref in (mine_ref, got_ref):
        extra = ref[groups:]
        norm = math.sqrt(CT * L) * lax.rsqrt(pick(extra, gather))[:1]
        scale = lax.rsqrt(extra + epsilon)
        scales = []
        for tile in range(2 * tiles):
            columns = []
            for phase in (2 * tile, 2 * tile + 1):
                if half >= 8:
                    count = half // 8
                    pieces = [scale[:, 2 * phases * k + phase :][:, :1] for k in range(2 * count)]
                    columns.append(
                        jnp.concatenate(
                            [jnp.where(first, pieces[k], pieces[k + count]) for k in range(count)], axis=0
                        )
                    )
                else:
                    columns.append(
                        jnp.where(first, scale[:half, phase : phase + 1], scale[half : 2 * half, phase : phase + 1])
                    )
            scales.append(jnp.where(low, columns[0], columns[1]) * norm)
        sides.append(scales)
    for tile in range(tiles):
        rows = slice(tile * half, (tile + 1) * half)
        mine_scale[rows] = sides[0][tiles + tile]
        got_scale[rows] = sides[1][tiles + tile]
        even_ref[rows], odd_ref[rows] = woven(
            straight, mine_ref[rows] * sides[0][tile], got_ref[rows] * sides[1][tile]
        )


def scaled(mine, got, phases, devices):
    half = jax.ShapeDtypeStruct((LANES // 2, LANES), f32)
    return pl.pallas_call(
        lambda *refs: scale_kernel(*refs, phases=phases, devices=devices),
        out_shape=(half,) * 4,
        in_specs=[IN_VMEM, IN_VMEM],
        out_specs=(IN_VMEM,) * 4,
        compiler_params=SMALL,
        cost_estimate=pl.CostEstimate(flops=2**32, bytes_accessed=2**18, transcendentals=0),
        name="scale",
    )(mine, got)


def finish_kernel(even_ref, odd_ref, mine_scale, got_scale, mine_ref, got_ref, out_ref, *, phases, devices):
    half = L // phases // 2
    tiles = phases // 4
    straight = panel_of(lax.axis_index("win"), devices) == 0
    mine = mine_ref[...] * mine_scale[...]
    got = got_ref[...] * got_scale[...]
    even, odd = woven(straight, mine, got)
    for tile in range(tiles):
        rows = slice(tile * half, (tile + 1) * half)
        for phase, value in enumerate((even_ref[rows], odd_ref[rows])):
            out_ref[pl.ds(2 * tile + phase, half, stride=phases), :] = value
        for phase, value in enumerate((even[rows], odd[rows])):
            out_ref[pl.ds(2 * (tiles + tile) + phase, half, stride=phases), :] = value


def finish(first, second, phases, devices):
    return pl.pallas_call(
        lambda *refs: finish_kernel(*refs, phases=phases, devices=devices),
        out_shape=jax.ShapeDtypeStruct((L // 2, LANES), f32),
        in_specs=[IN_VMEM] * 6,
        out_specs=IN_VMEM,
        compiler_params=SMALL,
        cost_estimate=pl.CostEstimate(flops=2**18, bytes_accessed=2**18, transcendentals=0),
        name="finish",
    )(*first, *second)


def masks_kernel(start_hbm, routed_ref, start_ref, sem, *, devices):
    copy = pltpu.make_async_copy(start_hbm, start_ref, sem)
    copy.start()
    held = routed_ref.shape[1]
    me = lax.axis_index("win")
    mine = panel_of(me, devices)
    per_chip = 2 * CT // devices
    row = iota((CT, held), 0)
    panels = (1 - mine, mine)
    channels = []
    for panel in panels:
        target = jnp.bitwise_xor(target_of(row // per_chip, panel, devices), me // 2)
        core = jnp.bitwise_xor(panel, panel_of(2 * target, devices))
        channel = target * per_chip + (row % per_chip + per_chip // 2 * core) % per_chip
        channels.append(channel - me * held - iota((CT, held), 1))
    copy.wait()
    for i, panel in enumerate(panels):
        routed_ref[i * CT : (i + 1) * CT] = (channels[i] + start_ref[panel] == 0).astype(f32).astype(bf16)


def masks(panel_start, held, devices):
    return pl.pallas_call(
        lambda *refs: masks_kernel(*refs, devices=devices),
        out_shape=jax.ShapeDtypeStruct((2 * CT, held), bf16),
        in_specs=[pl.BlockSpec(memory_space=pltpu.HBM)],
        out_specs=IN_VMEM,
        scratch_shapes=[pltpu.SMEM(panel_start.shape, jnp.int32), pltpu.SemaphoreType.DMA],
        compiler_params=SMALL,
        cost_estimate=pl.CostEstimate(flops=2**31, bytes_accessed=2**16, transcendentals=0),
        name="masks",
    )(panel_start)


def select_kernel(records_ref, routed_ref, away_ref, home_ref, *, begin):
    both = dot(routed_ref[...], records_ref[:, begin : begin + away_ref.shape[1]]).astype(bf16)
    away_ref[...] = both[:CT]
    home_ref[...] = both[CT:]


def selected(records, routed, begin, end):
    out = jax.ShapeDtypeStruct((CT, end - begin), bf16)
    return pl.pallas_call(
        lambda *refs: select_kernel(*refs, begin=begin),
        out_shape=(out, out),
        in_specs=[IN_VMEM, IN_VMEM],
        out_specs=(IN_VMEM, IN_VMEM),
        compiler_params=pltpu.CompilerParams(vmem_limit_bytes=SPARE),
        cost_estimate=pl.CostEstimate(flops=2**27, bytes_accessed=2**21, transcendentals=0),
        name="select",
    )(records, routed)


def add_kernel(kept_ref, got_ref, *refs):
    keep_ref, send_ref = refs[-2:]
    half = keep_ref.shape[0]
    keep_ref[...] = kept_ref[:half] + got_ref[:half]
    send_ref[...] = kept_ref[half:] + got_ref[half:]


def added(kept, got, *before):
    half = kept.shape[0] // 2
    if kept.dtype == bf16 and half % 16:
        whole = kept + got
        return whole[:half], whole[half:]
    part = jax.ShapeDtypeStruct((half, *kept.shape[1:]), kept.dtype)
    return pl.pallas_call(
        add_kernel,
        out_shape=(part, part),
        in_specs=[IN_VMEM, IN_VMEM] + [pl.BlockSpec(memory_space=pl.ANY)] * len(before),
        out_specs=(IN_VMEM, IN_VMEM),
        compiler_params=SMALL,
        cost_estimate=pl.CostEstimate(flops=2**32, bytes_accessed=2**20, transcendentals=0),
        name="add",
    )(kept, got, *before)


def local(records, templates, panel_start):
    devices = lax.axis_size("win")
    panel = panel_of(lax.axis_index("win"), devices)
    phases = devices // 2
    pairs = (L // phases + 2) // 2
    orders = bits_of(devices)
    steps = len(orders[0])

    def sibling(value):
        return lax.ppermute(value, "win", [(d, d ^ 1) for d in range(devices)])

    def exchange(value, step):
        return lax.ppermute(value, "win", [(d, d ^ 1 ^ orders[panel_of(d, devices)][step]) for d in range(devices)])

    def scattered(keep, send, until, before=()):
        for step in range(until - 1):
            keep, send = added(keep, exchange(send, step), *(before if step == 0 else ()))
        return keep, exchange(send, until - 1)

    half = records.shape[1] // 2
    routed = masks(panel_start, records.shape[0], devices)
    away_late, home_late = selected(records, routed, half, 2 * half)
    got_late = sibling(away_late)
    away_early, home_early = selected(records, routed, 0, half)
    got_early = sibling(away_early)

    keep, send = added(home_late, got_late)
    late = keep, send
    got_early, templates = lax.optimization_barrier((got_early, templates))
    early = added(home_early, got_early, keep)
    given = lax.dynamic_index_in_dim(templates, 1 - panel, 0, keepdims=False)
    w, norm = shifted(templates, sibling(given), phases, pairs)
    late = scattered(*late, steps)
    early = scattered(*early, steps, [norm])
    rest_rows, rest_energy, late_slide, rest_acc = correlate_late(late, w, phases)
    send_a, keep_a, early_slide = correlate_early(early, w, norm, (rest_rows, rest_energy, rest_acc), phases, devices)
    rows = [piece[0].shape[1] // phases for piece in (early, late)]
    send_b, keep_b = correlate_rest(early_slide, late_slide, w, rows, phases, devices)

    mine, other = halves(*scattered(keep_a, send_a, steps, [send_b]), phases)
    first = scaled(mine, sibling(other), phases, devices)
    mine, other = halves(*scattered(keep_b, send_b, steps), phases)
    return finish(first, (mine, sibling(other)), phases, devices)


def solution(mesh):
    placed = (P("win", "parts"), P(None, None, "win", None), P("parts"))
    return jax.shard_map(
        local, mesh=mesh, in_specs=placed, out_specs=P(("parts", "win"), None), check_vma=False
    )
```

```python
import math

import jax
import jax.numpy as jnp
from jax import lax
from jax.experimental import pallas as pl
from jax.experimental.pallas import tpu as pltpu
from jax.sharding import PartitionSpec as P

CT = 128
L = 512
LANES = 128
epsilon = 1e-06
f32 = jnp.float32
bf16 = jnp.bfloat16
SPARE = 12 * 2**20
IN_VMEM = pl.BlockSpec(memory_space=pltpu.VMEM)
SMALL = pltpu.CompilerParams(vmem_limit_bytes=8 * 2**20)


def iota(shape, dim):
    return lax.broadcasted_iota(jnp.int32, shape, dim)


def dot(a, b, dims=(((1,), (0,)), ((), ()))):
    return lax.dot_general(a, b, dims, preferred_element_type=f32)


def split3(v):
    high = v.astype(bf16)
    rest = v - high.astype(f32)
    middle = rest.astype(bf16)
    return high, middle, (rest - middle.astype(f32)).astype(bf16)


def pick(v, m):
    return sum(dot(part, m) for part in split3(v))


def picked(m, v):
    return sum(dot(m, part) for part in split3(v))


def give_kernel(templates_hbm, before, out_ref, sem, *, devices):
    panel = panel_of(lax.axis_index("win"), devices)
    copy = pltpu.make_async_copy(templates_hbm.at[1 - panel], out_ref, sem)
    copy.start()
    copy.wait()


def given(templates, before, devices):
    return pl.pallas_call(
        lambda *refs: give_kernel(*refs, devices=devices),
        out_shape=jax.ShapeDtypeStruct(templates.shape[1:], bf16),
        in_specs=[pl.BlockSpec(memory_space=pltpu.HBM), pl.BlockSpec(memory_space=pl.ANY)],
        out_specs=IN_VMEM,
        scratch_shapes=[pltpu.SemaphoreType.DMA],
        compiler_params=SMALL,
        cost_estimate=pl.CostEstimate(flops=2**28, bytes_accessed=2**20, transcendentals=0),
        name="give",
    )(templates, before)


def shift_kernel(templates_ref, other_ref, *refs, phases, devices):
    w_ref, norm_ref, rows_ref = refs[-3:]
    gc = other_ref.shape[0]
    panel = panel_of(lax.axis_index("win"), devices)
    groups = LANES // 2
    each = gc // groups
    channels = 2 * each
    versions, total, _ = w_ref.shape
    pad = channels * phases
    front = rows_ref.shape[0] - total
    rows_ref[pl.ds(0, front + pad), :] = jnp.zeros((front + pad, LANES), f32)
    rows_ref[pl.ds(front + pad + L * channels, total - pad - L * channels), :] = jnp.zeros(
        (total - pad - L * channels, LANES), f32
    )
    norm = jnp.zeros((1, LANES), f32)
    width = min(2, each) * LANES
    row, lane = iota((gc, width), 0), iota((gc, width), 1)
    for side, ref in enumerate((templates_ref.at[panel], other_ref)):
        for c in range(0, each, width // LANES):
            choose = (row == (lane % groups) * each + c + lane // LANES).astype(f32).astype(bf16)
            piece = dot(ref[...], choose, (((0,), (0,)), ((), ())))
            for i in range(width // LANES):
                one = piece[:, i * LANES : (i + 1) * LANES]
                norm = norm + jnp.sum(one * one, axis=0, keepdims=True)
                rows_ref[pl.ds(front + pad + side * each + c + i, L, stride=channels), :] = one
    norm_ref[...] = jnp.broadcast_to(norm, norm_ref.shape)
    low = iota((256, LANES), 1) < groups
    for v in range(versions):
        for at in range(0, total, 256):
            size = min(256, total - at)
            start = front + at - 2 * channels * v
            even = rows_ref[pl.ds(start, size), :]
            odd = rows_ref[pl.ds(start - channels, size), :]
            w_ref[v, at : at + size, :] = jnp.where(low[:size], even, odd).astype(bf16)


def shifted(templates, other, phases, pairs, *before):
    gc = other.shape[0]
    channels = 2 * gc // 64
    versions = max(1, 8 // channels)
    total = 256 * pairs + channels * phases
    front = (2 * versions - 1) * channels + 8
    front = (front + 7) // 8 * 8
    return pl.pallas_call(
        lambda *refs: shift_kernel(*refs, phases=phases, devices=2 * phases),
        in_specs=[IN_VMEM, IN_VMEM] + [pl.BlockSpec(memory_space=pl.ANY)] * len(before),
        out_specs=(IN_VMEM, IN_VMEM),
        out_shape=(
            jax.ShapeDtypeStruct((versions, total, LANES), bf16),
            jax.ShapeDtypeStruct((8, LANES), f32),
        ),
        scratch_shapes=[pltpu.VMEM((front + total, LANES), f32)],
        compiler_params=pltpu.CompilerParams(vmem_limit_bytes=512 * (front + total) + SPARE),
        cost_estimate=pl.CostEstimate(flops=2**28, bytes_accessed=2**20, transcendentals=0),
        name="shift_templates",
    )(templates, other, *before)


def bits_of(devices):
    x, z, *rest = [1 << i for i in range(1, devices.bit_length() - 1)]
    return [x, z] + rest, [z, x] + rest


def panel_of(device, devices):
    return sum(device >> i & 1 for i in range(devices.bit_length() - 1)) % 2


def target_of(slot, panel, devices):
    mine, theirs = bits_of(devices)
    chip = jnp.zeros_like(slot)
    for i, (p, q) in enumerate(zip(mine, theirs)):
        chip += (slot >> (len(mine) - 1 - i) & 1) * jnp.where(panel == 0, p, q)
    return chip // 2


def spread(pieces, spread_ref, phases):
    value = sum(r[...] for r in pieces[1:]) + pieces[0][...]
    channels, t = value.shape
    repeat = (iota((channels, LANES), 0) == iota((channels, LANES), 1) % channels).astype(f32).astype(bf16)
    spread_ref[...] = dot(value, repeat, (((0,), (0,)), ((), ())))
    count = t // phases
    phase = iota((count, LANES), 1) // channels
    rows = jnp.zeros((count, LANES), f32)
    for k in range(phases):
        rows = jnp.where(phase == k, spread_ref[pl.ds(k, count, stride=phases), :], rows)
    return rows


def fill_slide(rows_ref, slide_ref):
    span = slide_ref.shape[1]
    for k in range(slide_ref.shape[0]):
        slide_ref[k, :, 0:LANES] = rows_ref[pl.ds(2 * k, span), :].astype(bf16)
        slide_ref[k, :, LANES:] = rows_ref[pl.ds(2 * k + 1, span), :].astype(bf16)


def energies(squares, m, phases):
    n = squares.shape[0]
    channels = LANES // phases
    per = L // phases
    left, right = iota((LANES, LANES), 0) // channels, iota((LANES, LANES), 1) % (2 * phases)
    inside = right < phases
    tail = (inside & (left >= right)).astype(f32).astype(bf16)
    head = (inside & (left < right)).astype(f32).astype(bf16)
    sums = jnp.broadcast_to(jnp.sum(squares, axis=1, keepdims=True), squares.shape)
    distance = iota((m, n), 1) - iota((m, n), 0)
    band = ((distance >= 1) & (distance < per)).astype(f32).astype(bf16)
    begin = pick(squares[per : min(n, per + m)], head)
    if per + m > n:
        begin = jnp.concatenate([begin, jnp.zeros((per + m - n, LANES), f32)], axis=0)
    return pick(squares[:m], tail) + picked(band, sums) + begin


def correlate_tiles(slides, w_ref, acc_ref, tiles, phases):
    versions = w_ref.shape[0]
    channels = LANES // phases
    pairs = (w_ref.shape[1] - LANES) // 256
    m = sum(count for _, count in slides)

    def shifts(q, tile):
        v = tile % versions
        return w_ref[v, pl.ds(LANES + 256 * q - 2 * channels * (tile - v), 256), :]

    for q in range(pairs):
        window = [slide[q % 8, pl.ds(16 * (q // 8), count), :] for slide, count in slides]
        window = window[0] if len(window) == 1 else jnp.concatenate(window, axis=0)
        term = dot(window, jnp.concatenate([shifts(q, tile) for tile in tiles], axis=1))
        if q == 0:
            acc_ref[pl.ds(0, m), :] = term
        else:
            acc_ref[pl.ds(0, m), :] += term


def late_kernel(*refs, phases):
    *pieces, w_ref, out_rows, out_energy, out_acc, spread_ref, rows_ref, slide_ref = refs
    rows = spread(pieces, spread_ref, phases)
    count = rows.shape[0]
    out_rows[...] = rows
    rows_ref[pl.ds(0, count), :] = rows
    rows_ref[pl.ds(count, rows_ref.shape[0] - count), :] = jnp.zeros((rows_ref.shape[0] - count, LANES), f32)
    fill_slide(rows_ref, slide_ref)
    out_energy[...] = energies(rows * rows, count, phases)
    correlate_tiles([(slide_ref, count)], w_ref, out_acc, range(phases // 2), phases)


def write_blocks(send_ref, keep_ref, acc_ref, lead, per, devices):
    me = lax.axis_index("win")
    kept = keep_ref.shape[0]
    for slot in range(2 * kept):
        chip = jnp.bitwise_xor(me // 2, target_of(jnp.int32(slot), panel_of(me, devices), devices))
        at = pl.multiple_of(chip * per, 8)
        ref = keep_ref if slot < kept else send_ref
        for tile in range(acc_ref.shape[1] // LANES):
            ref[slot % kept, tile * per : (tile + 1) * per, :] = acc_ref[
                pl.ds(at, per), tile * LANES : (tile + 1) * LANES
            ]
        if lead is not None:
            ref[slot % kept, LANES:, :] = lead(at)


def early_kernel(*refs, phases, devices):
    *pieces, w_ref, norm_ref, rest_rows, rest_energy, rest_acc = refs[: len(refs) - 7]
    send_ref, keep_ref, slide_ref, rows_ref, spread_ref, energy_ref, acc_ref = refs[len(refs) - 7 :]
    rows = spread(pieces, spread_ref, phases)
    m = rows.shape[0]
    n = m + rest_rows.shape[0]
    rows_ref[pl.ds(0, m), :] = rows
    rows_ref[pl.ds(m, n - m), :] = rest_rows[...]
    fill_slide(rows_ref, slide_ref)
    acc_ref[pl.ds(m, n - m), :] = rest_acc[:, : acc_ref.shape[1]]
    correlate_tiles([(slide_ref, m)], w_ref, acc_ref, range(phases // 4), phases)

    squares = rows_ref[...]
    energy_ref[pl.ds(0, m), :] = energies(squares * squares, m, phases)
    energy_ref[pl.ds(m, n - m), :] = rest_energy[...]
    per = L // phases
    place = iota((LANES, LANES), 1)
    wanted = (place // (2 * phases)) * phases + place % (2 * phases) - phases
    scatter = ((place % (2 * phases) >= phases) & (iota((LANES, LANES), 0) == wanted)).astype(f32).astype(bf16)
    norm = pick(norm_ref[...], scatter)
    lane = iota((8, LANES), 1)

    def extras(at):
        e = norm
        for k in range(per // 8):
            e = jnp.where(
                (lane // (2 * phases) == k) & (lane % (2 * phases) < phases), energy_ref[pl.ds(at + 8 * k, 8), :], e
            )
        return e

    write_blocks(send_ref, keep_ref, acc_ref, extras, per, devices)


def rest_kernel(slide_ref, w_ref, rest_acc, send_ref, keep_ref, acc_ref, *, phases, devices):
    n, width = acc_ref.shape
    m = n - rest_acc.shape[0]
    acc_ref[pl.ds(m, n - m), :] = rest_acc[:, width:]
    correlate_tiles([(slide_ref, m)], w_ref, acc_ref, range(phases // 4, phases // 2), phases)
    write_blocks(send_ref, keep_ref, acc_ref, None, L // phases, devices)


def grant(shapes):
    return pltpu.CompilerParams(vmem_limit_bytes=sum(math.prod(s.shape) * 4 for s in shapes) + SPARE)


def slide_shape(m, phases):
    pairs = (L // phases + 2) // 2
    return (min(8, pairs), m + 16 * ((pairs - 1) // 8), 256)


def correlate_late(pieces, w, phases):
    t = pieces[0].shape[1]
    count = t // phases
    slide = slide_shape(count, phases)
    shapes = [pltpu.VMEM((t, LANES), f32), pltpu.VMEM((slide[1] + 16, LANES), f32), pltpu.VMEM(slide, bf16)]
    return pl.pallas_call(
        lambda *refs: late_kernel(*refs, phases=phases),
        out_shape=(
            jax.ShapeDtypeStruct((count, LANES), f32),
            jax.ShapeDtypeStruct((count, LANES), f32),
            jax.ShapeDtypeStruct((count, phases * 64), f32),
        ),
        in_specs=[IN_VMEM] * (len(pieces) + 1),
        out_specs=(IN_VMEM,) * 3,
        scratch_shapes=shapes,
        compiler_params=grant(shapes),
        cost_estimate=pl.CostEstimate(flops=2**31, bytes_accessed=2**22, transcendentals=0),
        name="correlate_late",
    )(*pieces, w)


def correlate_early(pieces, w, norm, rest, phases, devices):
    t = pieces[0].shape[1]
    m = t // phases
    n = m + rest[0].shape[0]
    shapes = [
        pltpu.VMEM((n, LANES), f32),
        pltpu.VMEM((t, LANES), f32),
        pltpu.VMEM((n, LANES), f32),
        pltpu.VMEM((n, phases * 32), f32),
    ]
    block = jax.ShapeDtypeStruct((devices // 4, LANES + 8, LANES), f32)
    return pl.pallas_call(
        lambda *refs: early_kernel(*refs, phases=phases, devices=devices),
        out_shape=(block, block, jax.ShapeDtypeStruct(slide_shape(m, phases), bf16)),
        in_specs=[IN_VMEM] * (len(pieces) + 5),
        out_specs=(IN_VMEM,) * 3,
        scratch_shapes=shapes,
        compiler_params=grant(shapes),
        cost_estimate=pl.CostEstimate(flops=2**32, bytes_accessed=2**24, transcendentals=0),
        name="correlate_early",
    )(*pieces, w, norm, *rest)


def correlate_rest(slide, w, rest_acc, m, phases, devices):
    shapes = [pltpu.VMEM((m + rest_acc.shape[0], phases * 32), f32)]
    block = jax.ShapeDtypeStruct((devices // 4, LANES, LANES), f32)
    return pl.pallas_call(
        lambda *refs: rest_kernel(*refs, phases=phases, devices=devices),
        out_shape=(block, block),
        in_specs=[IN_VMEM] * 3,
        out_specs=(IN_VMEM, IN_VMEM),
        scratch_shapes=shapes,
        compiler_params=grant(shapes),
        cost_estimate=pl.CostEstimate(flops=2**33, bytes_accessed=2**24, transcendentals=0),
        name="correlate_rest",
    )(slide, w, rest_acc)


def cut(block, phases):
    per = L // phases
    half = per // 2
    starts = range(0, LANES, per)
    return (
        jnp.concatenate([block[at : at + half] for at in starts], axis=0),
        jnp.concatenate([block[at + half : at + per] for at in starts], axis=0),
    )


def halves_kernel(kept_ref, got_ref, mine_ref, other_ref, *, phases):
    first = lax.axis_index("win") % 2 == 0
    block = kept_ref[0] + got_ref[0]
    lower, upper = cut(block, phases)
    rows = LANES // 2
    mine_ref[0:rows] = jnp.where(first, lower, upper)
    other_ref[0:rows] = jnp.where(first, upper, lower)
    if block.shape[0] > LANES:
        mine_ref[rows:] = block[LANES:]
        other_ref[rows:] = block[LANES:]


def halves(kept, got, phases):
    half = jax.ShapeDtypeStruct((kept.shape[1] - LANES // 2, LANES), f32)
    return pl.pallas_call(
        lambda *refs: halves_kernel(*refs, phases=phases),
        out_shape=(half, half),
        in_specs=[IN_VMEM, IN_VMEM],
        out_specs=(IN_VMEM, IN_VMEM),
        compiler_params=SMALL,
        cost_estimate=pl.CostEstimate(flops=2**32, bytes_accessed=2**20, transcendentals=0),
        name="halves",
    )(kept, got)


def woven(straight, mine, got):
    groups = LANES // 2
    low = iota(mine.shape, 1) < groups
    zero, one = jnp.where(straight, mine, got), jnp.where(straight, got, mine)
    return jnp.where(low, zero, pltpu.roll(one, groups, 1)), jnp.where(low, pltpu.roll(zero, groups, 1), one)


def scale_kernel(mine_ref, got_ref, even_ref, odd_ref, mine_scale, got_scale, *, phases, devices):
    groups = LANES // 2
    per = L // phases
    half = per // 2
    tiles = phases // 4
    me = lax.axis_index("win")
    first = me % 2 == 0
    straight = panel_of(me, devices) == 0
    place = iota((LANES, LANES), 0)
    wanted = (place // (2 * phases)) * phases + place % (2 * phases) - phases
    gather = (
        ((place % (2 * phases) >= phases) & (iota((LANES, LANES), 1) % groups == wanted)).astype(f32).astype(bf16)
    )
    low = iota((half, LANES), 1) < groups
    sides = []
    for ref in (mine_ref, got_ref):
        extra = ref[groups:]
        norm = math.sqrt(CT * L) * lax.rsqrt(pick(extra, gather))[:1]
        scale = lax.rsqrt(extra + epsilon)
        scales = []
        for tile in range(2 * tiles):
            columns = []
            for phase in (2 * tile, 2 * tile + 1):
                if half >= 8:
                    count = half // 8
                    pieces = [scale[:, 2 * phases * k + phase :][:, :1] for k in range(2 * count)]
                    columns.append(
                        jnp.concatenate(
                            [jnp.where(first, pieces[k], pieces[k + count]) for k in range(count)], axis=0
                        )
                    )
                else:
                    columns.append(
                        jnp.where(first, scale[:half, phase : phase + 1], scale[half : 2 * half, phase : phase + 1])
                    )
            scales.append(jnp.where(low, columns[0], columns[1]) * norm)
        sides.append(scales)
    for tile in range(tiles):
        rows = slice(tile * half, (tile + 1) * half)
        mine_scale[rows] = sides[0][tiles + tile]
        got_scale[rows] = sides[1][tiles + tile]
        even_ref[rows], odd_ref[rows] = woven(
            straight, mine_ref[rows] * sides[0][tile], got_ref[rows] * sides[1][tile]
        )


def scaled(mine, got, phases, devices):
    half = jax.ShapeDtypeStruct((LANES // 2, LANES), f32)
    return pl.pallas_call(
        lambda *refs: scale_kernel(*refs, phases=phases, devices=devices),
        out_shape=(half,) * 4,
        in_specs=[IN_VMEM, IN_VMEM],
        out_specs=(IN_VMEM,) * 4,
        compiler_params=SMALL,
        cost_estimate=pl.CostEstimate(flops=2**32, bytes_accessed=2**18, transcendentals=0),
        name="scale",
    )(mine, got)


def finish_kernel(even_ref, odd_ref, mine_scale, got_scale, mine_ref, got_ref, out_ref, *, phases, devices):
    half = L // phases // 2
    tiles = phases // 4
    straight = panel_of(lax.axis_index("win"), devices) == 0
    mine = mine_ref[...] * mine_scale[...]
    got = got_ref[...] * got_scale[...]
    even, odd = woven(straight, mine, got)
    for tile in range(tiles):
        rows = slice(tile * half, (tile + 1) * half)
        for phase, value in enumerate((even_ref[rows], odd_ref[rows])):
            out_ref[pl.ds(2 * tile + phase, half, stride=phases), :] = value
        for phase, value in enumerate((even[rows], odd[rows])):
            out_ref[pl.ds(2 * (tiles + tile) + phase, half, stride=phases), :] = value


def finish(first, second, phases, devices):
    return pl.pallas_call(
        lambda *refs: finish_kernel(*refs, phases=phases, devices=devices),
        out_shape=jax.ShapeDtypeStruct((L // 2, LANES), f32),
        in_specs=[IN_VMEM] * 6,
        out_specs=IN_VMEM,
        compiler_params=SMALL,
        cost_estimate=pl.CostEstimate(flops=2**18, bytes_accessed=2**18, transcendentals=0),
        name="finish",
    )(*first, *second)


def masks_kernel(start_hbm, routed_ref, start_ref, sem, *, devices):
    copy = pltpu.make_async_copy(start_hbm, start_ref, sem)
    copy.start()
    held = routed_ref.shape[1]
    me = lax.axis_index("win")
    mine = panel_of(me, devices)
    per_chip = 2 * CT // devices
    row = iota((CT, held), 0)
    panels = (1 - mine, mine)
    channels = []
    for panel in panels:
        target = jnp.bitwise_xor(target_of(row // per_chip, panel, devices), me // 2)
        core = jnp.bitwise_xor(panel, panel_of(2 * target, devices))
        channel = target * per_chip + (row % per_chip + per_chip // 2 * core) % per_chip
        channels.append(channel - me * held - iota((CT, held), 1))
    copy.wait()
    for i, panel in enumerate(panels):
        routed_ref[i * CT : (i + 1) * CT] = (channels[i] + start_ref[panel] == 0).astype(f32).astype(bf16)


def masks(panel_start, held, devices):
    return pl.pallas_call(
        lambda *refs: masks_kernel(*refs, devices=devices),
        out_shape=jax.ShapeDtypeStruct((2 * CT, held), bf16),
        in_specs=[pl.BlockSpec(memory_space=pltpu.HBM)],
        out_specs=IN_VMEM,
        scratch_shapes=[pltpu.SMEM(panel_start.shape, jnp.int32), pltpu.SemaphoreType.DMA],
        compiler_params=SMALL,
        cost_estimate=pl.CostEstimate(flops=2**31, bytes_accessed=2**16, transcendentals=0),
        name="masks",
    )(panel_start)


def select_kernel(records_ref, routed_ref, *refs, begin):
    away_ref, home_ref = refs[-2:]
    both = dot(routed_ref[...], records_ref[:, begin : begin + away_ref.shape[1]]).astype(bf16)
    away_ref[...] = both[:CT]
    home_ref[...] = both[CT:]


def selected(records, routed, begin, end, *before):
    out = jax.ShapeDtypeStruct((CT, end - begin), bf16)
    return pl.pallas_call(
        lambda *refs: select_kernel(*refs, begin=begin),
        out_shape=(out, out),
        in_specs=[IN_VMEM, IN_VMEM] + [pl.BlockSpec(memory_space=pl.ANY)] * len(before),
        out_specs=(IN_VMEM, IN_VMEM),
        compiler_params=pltpu.CompilerParams(vmem_limit_bytes=SPARE),
        cost_estimate=pl.CostEstimate(flops=2**27, bytes_accessed=2**21, transcendentals=0),
        name="select",
    )(records, routed, *before)


def add_kernel(kept_ref, got_ref, *refs):
    keep_ref, send_ref = refs[-2:]
    half = keep_ref.shape[0]
    keep_ref[...] = kept_ref[:half] + got_ref[:half]
    send_ref[...] = kept_ref[half:] + got_ref[half:]


def added(kept, got, *before):
    half = kept.shape[0] // 2
    if kept.dtype == bf16 and half % 16:
        whole = kept + got
        return whole[:half], whole[half:]
    part = jax.ShapeDtypeStruct((half, *kept.shape[1:]), kept.dtype)
    return pl.pallas_call(
        add_kernel,
        out_shape=(part, part),
        in_specs=[IN_VMEM, IN_VMEM] + [pl.BlockSpec(memory_space=pl.ANY)] * len(before),
        out_specs=(IN_VMEM, IN_VMEM),
        compiler_params=SMALL,
        cost_estimate=pl.CostEstimate(flops=2**32, bytes_accessed=2**20, transcendentals=0),
        name="add",
    )(kept, got, *before)


def local(records, templates, panel_start):
    devices = lax.axis_size("win")
    panel = panel_of(lax.axis_index("win"), devices)
    phases = devices // 2
    pairs = (L // phases + 2) // 2
    orders = bits_of(devices)
    steps = len(orders[0])

    def sibling(value):
        return lax.ppermute(value, "win", [(d, d ^ 1) for d in range(devices)])

    def exchange(value, step):
        return lax.ppermute(value, "win", [(d, d ^ 1 ^ orders[panel_of(d, devices)][step]) for d in range(devices)])

    def scattered(keep, send, until, before=()):
        for step in range(until - 1):
            keep, send = added(keep, exchange(send, step), *(before if step == 0 else ()))
        return keep, exchange(send, until - 1)

    half = records.shape[1] // 2
    routed = masks(panel_start, records.shape[0], devices)
    away_late, home_late = selected(records, routed, half, 2 * half)
    got_late = sibling(away_late)
    away_early, home_early = selected(records, routed, 0, half, away_late)
    got_early = sibling(away_early)

    templates = templates.reshape(templates.shape[0], -1, L)
    other = sibling(given(templates, away_early, devices))
    late = added(home_late, got_late)
    early = added(home_early, got_early, late[0])
    w, norm = shifted(templates, other, phases, pairs, early[0])
    for step in range(steps - 1):
        late = added(late[0], exchange(late[1], step), *([norm] if step == 0 else []))
        early = added(early[0], exchange(early[1], step))
    late, early = [(keep, exchange(send, steps - 1)) for keep, send in (late, early)]
    rest_rows, rest_energy, rest_acc = correlate_late(late, w, phases)
    send_a, keep_a, slide = correlate_early(early, w, norm, (rest_rows, rest_energy, rest_acc), phases, devices)
    send_b, keep_b = correlate_rest(slide, w, rest_acc, half // phases, phases, devices)

    mine, other = halves(*scattered(keep_a, send_a, steps, [send_b]), phases)
    first = scaled(mine, sibling(other), phases, devices)
    mine, other = halves(*scattered(keep_b, send_b, steps), phases)
    return finish(first, (mine, sibling(other)), phases, devices)


def solution(mesh):
    placed = (P("win", "parts"), P(None, None, "win", None), P("parts"))
    return jax.shard_map(
        local, mesh=mesh, in_specs=placed, out_specs=P(("parts", "win"), None), check_vma=False
    )
```

```python
import math

import jax
import jax.numpy as jnp
from jax import lax
from jax.experimental import pallas as pl
from jax.experimental.pallas import tpu as pltpu
from jax.sharding import PartitionSpec as P

CT = 128
L = 512
LANES = 128
epsilon = 1e-06
f32 = jnp.float32
bf16 = jnp.bfloat16
SPARE = 12 * 2**20
IN_VMEM = pl.BlockSpec(memory_space=pltpu.VMEM)
SMALL = pltpu.CompilerParams(vmem_limit_bytes=8 * 2**20)


def iota(shape, dim):
    return lax.broadcasted_iota(jnp.int32, shape, dim)


def dot(a, b, dims=(((1,), (0,)), ((), ()))):
    return lax.dot_general(a, b, dims, preferred_element_type=f32)


def split3(v):
    high = v.astype(bf16)
    rest = v - high.astype(f32)
    middle = rest.astype(bf16)
    return high, middle, (rest - middle.astype(f32)).astype(bf16)


def pick(v, m):
    return sum(dot(part, m) for part in split3(v))


def picked(m, v):
    return sum(dot(m, part) for part in split3(v))


def give_kernel(templates_hbm, before, out_ref, sem, *, devices):
    panel = panel_of(lax.axis_index("win"), devices)
    copy = pltpu.make_async_copy(templates_hbm.at[1 - panel], out_ref, sem)
    copy.start()
    copy.wait()


def given(templates, before, devices):
    return pl.pallas_call(
        lambda *refs: give_kernel(*refs, devices=devices),
        out_shape=jax.ShapeDtypeStruct(templates.shape[1:], bf16),
        in_specs=[pl.BlockSpec(memory_space=pltpu.HBM), pl.BlockSpec(memory_space=pl.ANY)],
        out_specs=IN_VMEM,
        scratch_shapes=[pltpu.SemaphoreType.DMA],
        compiler_params=SMALL,
        cost_estimate=pl.CostEstimate(flops=2**28, bytes_accessed=2**20, transcendentals=0),
        name="give",
    )(templates, before)


def shift_kernel(templates_ref, other_ref, *refs, phases, devices):
    w_ref, norm_ref, rows_ref = refs[-3:]
    gc = other_ref.shape[0]
    panel = panel_of(lax.axis_index("win"), devices)
    groups = LANES // 2
    each = gc // groups
    channels = 2 * each
    versions, total, _ = w_ref.shape
    pad = channels * phases
    front = rows_ref.shape[0] - total
    rows_ref[pl.ds(0, front + pad), :] = jnp.zeros((front + pad, LANES), f32)
    rows_ref[pl.ds(front + pad + L * channels, total - pad - L * channels), :] = jnp.zeros(
        (total - pad - L * channels, LANES), f32
    )
    norm = jnp.zeros((1, LANES), f32)
    width = min(2, each) * LANES
    row, lane = iota((gc, width), 0), iota((gc, width), 1)
    for side, ref in enumerate((templates_ref.at[panel], other_ref)):
        for c in range(0, each, width // LANES):
            choose = (row == (lane % groups) * each + c + lane // LANES).astype(f32).astype(bf16)
            piece = dot(ref[...], choose, (((0,), (0,)), ((), ())))
            for i in range(width // LANES):
                one = piece[:, i * LANES : (i + 1) * LANES]
                norm = norm + jnp.sum(one * one, axis=0, keepdims=True)
                rows_ref[pl.ds(front + pad + side * each + c + i, L, stride=channels), :] = one
    norm_ref[...] = jnp.broadcast_to(norm, norm_ref.shape)
    low = iota((256, LANES), 1) < groups
    for v in range(versions):
        for at in range(0, total, 256):
            size = min(256, total - at)
            start = front + at - 2 * channels * v
            even = rows_ref[pl.ds(start, size), :]
            odd = rows_ref[pl.ds(start - channels, size), :]
            w_ref[v, at : at + size, :] = jnp.where(low[:size], even, odd).astype(bf16)


def shifted(templates, other, phases, pairs, *before):
    gc = other.shape[0]
    channels = 2 * gc // 64
    versions = max(1, 8 // channels)
    total = 256 * pairs + channels * phases
    front = (2 * versions - 1) * channels + 8
    front = (front + 7) // 8 * 8
    return pl.pallas_call(
        lambda *refs: shift_kernel(*refs, phases=phases, devices=2 * phases),
        in_specs=[IN_VMEM, IN_VMEM] + [pl.BlockSpec(memory_space=pl.ANY)] * len(before),
        out_specs=(IN_VMEM, IN_VMEM),
        out_shape=(
            jax.ShapeDtypeStruct((versions, total, LANES), bf16),
            jax.ShapeDtypeStruct((8, LANES), f32),
        ),
        scratch_shapes=[pltpu.VMEM((front + total, LANES), f32)],
        compiler_params=pltpu.CompilerParams(vmem_limit_bytes=512 * (front + total) + SPARE),
        cost_estimate=pl.CostEstimate(flops=2**28, bytes_accessed=2**20, transcendentals=0),
        name="shift_templates",
    )(templates, other, *before)


def bits_of(devices):
    x, z, *rest = [1 << i for i in range(1, devices.bit_length() - 1)]
    return [x, z] + rest, [z, x] + rest


def panel_of(device, devices):
    return sum(device >> i & 1 for i in range(devices.bit_length() - 1)) % 2


def target_of(slot, panel, devices):
    mine, theirs = bits_of(devices)
    chip = jnp.zeros_like(slot)
    for i, (p, q) in enumerate(zip(mine, theirs)):
        chip += (slot >> (len(mine) - 1 - i) & 1) * jnp.where(panel == 0, p, q)
    return chip // 2


def spread(value, repeat, spread_ref, phases):
    t = value.shape[1]
    spread_ref[...] = dot(value, repeat, (((0,), (0,)), ((), ())))
    count = t // phases
    phase = iota((count, LANES), 1) // (LANES // phases)
    rows = jnp.zeros((count, LANES), f32)
    for k in range(phases):
        rows = jnp.where(phase == k, spread_ref[pl.ds(k, count, stride=phases), :], rows)
    return rows


def spread_pieces(pieces, spread_ref, phases):
    value = sum(r[...] for r in pieces[1:]) + pieces[0][...]
    channels = value.shape[0]
    repeat = (iota((channels, LANES), 0) == iota((channels, LANES), 1) % channels).astype(f32).astype(bf16)
    return spread(value, repeat, spread_ref, phases)


def fill_slide(rows_ref, slide_ref):
    span = slide_ref.shape[1]
    for k in range(slide_ref.shape[0]):
        slide_ref[k, :, 0:LANES] = rows_ref[pl.ds(2 * k, span), :].astype(bf16)
        slide_ref[k, :, LANES:] = rows_ref[pl.ds(2 * k + 1, span), :].astype(bf16)


def energies(squares, m, phases):
    n = squares.shape[0]
    channels = LANES // phases
    per = L // phases
    left, right = iota((LANES, LANES), 0) // channels, iota((LANES, LANES), 1) % (2 * phases)
    inside = right < phases
    tail = (inside & (left >= right)).astype(f32).astype(bf16)
    head = (inside & (left < right)).astype(f32).astype(bf16)
    sums = jnp.broadcast_to(jnp.sum(squares, axis=1, keepdims=True), squares.shape)
    distance = iota((m, n), 1) - iota((m, n), 0)
    band = ((distance >= 1) & (distance < per)).astype(f32).astype(bf16)
    begin = pick(squares[per : min(n, per + m)], head)
    if per + m > n:
        begin = jnp.concatenate([begin, jnp.zeros((per + m - n, LANES), f32)], axis=0)
    return pick(squares[:m], tail) + picked(band, sums) + begin


def energy_kernel(first_ref, second_ref, *refs, phases):
    out_ref, squares_ref, spread_ref = refs[-3:]
    squares = jnp.zeros((1, first_ref.shape[1]), f32)
    for ref in (first_ref, second_ref):
        value = ref[...].astype(f32)
        squares = squares + jnp.sum(value * value, axis=0, keepdims=True)
    parts = list(split3(squares)) + [jnp.zeros((13, squares.shape[1]), bf16)]
    repeat = ((iota((16, LANES), 1) % (LANES // phases) == 0) & (iota((16, LANES), 0) < 3)).astype(f32).astype(bf16)
    rows = spread(jnp.concatenate(parts, axis=0), repeat, spread_ref, phases)
    squares_ref[...] = rows
    following = [ref[...] for ref in refs[:-4]]
    out_ref[...] = energies(jnp.concatenate([rows] + following, axis=0), rows.shape[0], phases)


def energy_of(chunk, following, before, phases):
    t = chunk[0].shape[1]
    shapes = [pltpu.VMEM((t, LANES), f32)]
    out = jax.ShapeDtypeStruct((t // phases, LANES), f32)
    return pl.pallas_call(
        lambda *refs: energy_kernel(*refs, phases=phases),
        out_shape=(out, out),
        in_specs=[IN_VMEM] * (2 + len(following)) + [pl.BlockSpec(memory_space=pl.ANY)],
        out_specs=(IN_VMEM, IN_VMEM),
        scratch_shapes=shapes,
        compiler_params=grant(shapes),
        cost_estimate=pl.CostEstimate(flops=2**28, bytes_accessed=2**20, transcendentals=0),
        name="energy",
    )(*chunk, *following, before)


def correlate_tiles(slides, w_ref, acc_ref, tiles, phases):
    versions = w_ref.shape[0]
    channels = LANES // phases
    pairs = (w_ref.shape[1] - LANES) // 256
    m = sum(count for _, count in slides)

    def shifts(q, tile):
        v = tile % versions
        return w_ref[v, pl.ds(LANES + 256 * q - 2 * channels * (tile - v), 256), :]

    for q in range(pairs):
        window = [slide[q % 8, pl.ds(16 * (q // 8), count), :] for slide, count in slides]
        window = window[0] if len(window) == 1 else jnp.concatenate(window, axis=0)
        term = dot(window, jnp.concatenate([shifts(q, tile) for tile in tiles], axis=1))
        if q == 0:
            acc_ref[pl.ds(0, m), :] = term
        else:
            acc_ref[pl.ds(0, m), :] += term


def late_kernel(*refs, phases):
    *pieces, w_ref, out_rows, out_acc, spread_ref, rows_ref, slide_ref = refs
    rows = spread_pieces(pieces, spread_ref, phases)
    count = rows.shape[0]
    out_rows[...] = rows
    rows_ref[pl.ds(0, count), :] = rows
    rows_ref[pl.ds(count, rows_ref.shape[0] - count), :] = jnp.zeros((rows_ref.shape[0] - count, LANES), f32)
    fill_slide(rows_ref, slide_ref)
    correlate_tiles([(slide_ref, count)], w_ref, out_acc, range(phases // 2), phases)


def write_blocks(send_ref, keep_ref, acc_ref, lead, per, devices):
    me = lax.axis_index("win")
    kept = keep_ref.shape[0]
    for slot in range(2 * kept):
        chip = jnp.bitwise_xor(me // 2, target_of(jnp.int32(slot), panel_of(me, devices), devices))
        at = pl.multiple_of(chip * per, 8)
        ref = keep_ref if slot < kept else send_ref
        for tile in range(acc_ref.shape[1] // LANES):
            ref[slot % kept, tile * per : (tile + 1) * per, :] = acc_ref[
                pl.ds(at, per), tile * LANES : (tile + 1) * LANES
            ]
        if lead is not None:
            ref[slot % kept, LANES:, :] = lead(at)


def early_kernel(*refs, phases, devices):
    *pieces, w_ref, norm_ref, early_energy, late_energy, rest_rows, rest_acc = refs[: len(refs) - 7]
    send_ref, keep_ref, slide_ref, rows_ref, spread_ref, energy_ref, acc_ref = refs[len(refs) - 7 :]
    rows = spread_pieces(pieces, spread_ref, phases)
    m = rows.shape[0]
    n = m + rest_rows.shape[0]
    rows_ref[pl.ds(0, m), :] = rows
    rows_ref[pl.ds(m, n - m), :] = rest_rows[...]
    fill_slide(rows_ref, slide_ref)
    acc_ref[pl.ds(m, n - m), :] = rest_acc[:, : acc_ref.shape[1]]
    correlate_tiles([(slide_ref, m)], w_ref, acc_ref, range(phases // 4), phases)

    energy_ref[pl.ds(0, m), :] = early_energy[...]
    energy_ref[pl.ds(m, n - m), :] = late_energy[...]
    per = L // phases
    place = iota((LANES, LANES), 1)
    wanted = (place // (2 * phases)) * phases + place % (2 * phases) - phases
    scatter = ((place % (2 * phases) >= phases) & (iota((LANES, LANES), 0) == wanted)).astype(f32).astype(bf16)
    norm = pick(norm_ref[...], scatter)
    lane = iota((8, LANES), 1)

    def extras(at):
        e = norm
        for k in range(per // 8):
            e = jnp.where(
                (lane // (2 * phases) == k) & (lane % (2 * phases) < phases), energy_ref[pl.ds(at + 8 * k, 8), :], e
            )
        return e

    write_blocks(send_ref, keep_ref, acc_ref, extras, per, devices)


def rest_kernel(slide_ref, w_ref, rest_acc, send_ref, keep_ref, acc_ref, *, phases, devices):
    n, width = acc_ref.shape
    m = n - rest_acc.shape[0]
    acc_ref[pl.ds(m, n - m), :] = rest_acc[:, width:]
    correlate_tiles([(slide_ref, m)], w_ref, acc_ref, range(phases // 4, phases // 2), phases)
    write_blocks(send_ref, keep_ref, acc_ref, None, L // phases, devices)


def grant(shapes):
    return pltpu.CompilerParams(vmem_limit_bytes=sum(math.prod(s.shape) * 4 for s in shapes) + SPARE)


def slide_shape(m, phases):
    pairs = (L // phases + 2) // 2
    return (min(8, pairs), m + 16 * ((pairs - 1) // 8), 256)


def correlate_late(pieces, w, phases):
    t = pieces[0].shape[1]
    count = t // phases
    slide = slide_shape(count, phases)
    shapes = [pltpu.VMEM((t, LANES), f32), pltpu.VMEM((slide[1] + 16, LANES), f32), pltpu.VMEM(slide, bf16)]
    return pl.pallas_call(
        lambda *refs: late_kernel(*refs, phases=phases),
        out_shape=(
            jax.ShapeDtypeStruct((count, LANES), f32),
            jax.ShapeDtypeStruct((count, phases * 64), f32),
        ),
        in_specs=[IN_VMEM] * (len(pieces) + 1),
        out_specs=(IN_VMEM,) * 2,
        scratch_shapes=shapes,
        compiler_params=grant(shapes),
        cost_estimate=pl.CostEstimate(flops=2**31, bytes_accessed=2**22, transcendentals=0),
        name="correlate_late",
    )(*pieces, w)


def correlate_early(pieces, w, norm, energy, rest, phases, devices):
    t = pieces[0].shape[1]
    m = t // phases
    n = m + rest[0].shape[0]
    shapes = [
        pltpu.VMEM((n, LANES), f32),
        pltpu.VMEM((t, LANES), f32),
        pltpu.VMEM((n, LANES), f32),
        pltpu.VMEM((n, phases * 32), f32),
    ]
    block = jax.ShapeDtypeStruct((devices // 4, LANES + 8, LANES), f32)
    return pl.pallas_call(
        lambda *refs: early_kernel(*refs, phases=phases, devices=devices),
        out_shape=(block, block, jax.ShapeDtypeStruct(slide_shape(m, phases), bf16)),
        in_specs=[IN_VMEM] * (len(pieces) + 6),
        out_specs=(IN_VMEM,) * 3,
        scratch_shapes=shapes,
        compiler_params=grant(shapes),
        cost_estimate=pl.CostEstimate(flops=2**32, bytes_accessed=2**24, transcendentals=0),
        name="correlate_early",
    )(*pieces, w, norm, *energy, *rest)


def correlate_rest(slide, w, rest_acc, m, phases, devices):
    shapes = [pltpu.VMEM((m + rest_acc.shape[0], phases * 32), f32)]
    block = jax.ShapeDtypeStruct((devices // 4, LANES, LANES), f32)
    return pl.pallas_call(
        lambda *refs: rest_kernel(*refs, phases=phases, devices=devices),
        out_shape=(block, block),
        in_specs=[IN_VMEM] * 3,
        out_specs=(IN_VMEM, IN_VMEM),
        scratch_shapes=shapes,
        compiler_params=grant(shapes),
        cost_estimate=pl.CostEstimate(flops=2**33, bytes_accessed=2**24, transcendentals=0),
        name="correlate_rest",
    )(slide, w, rest_acc)


def cut(block, phases):
    per = L // phases
    half = per // 2
    starts = range(0, LANES, per)
    return (
        jnp.concatenate([block[at : at + half] for at in starts], axis=0),
        jnp.concatenate([block[at + half : at + per] for at in starts], axis=0),
    )


def halves_kernel(kept_ref, got_ref, mine_ref, other_ref, *, phases):
    first = lax.axis_index("win") % 2 == 0
    block = kept_ref[0] + got_ref[0]
    lower, upper = cut(block, phases)
    rows = LANES // 2
    mine_ref[0:rows] = jnp.where(first, lower, upper)
    other_ref[0:rows] = jnp.where(first, upper, lower)
    if block.shape[0] > LANES:
        mine_ref[rows:] = block[LANES:]
        other_ref[rows:] = block[LANES:]


def halves(kept, got, phases):
    half = jax.ShapeDtypeStruct((kept.shape[1] - LANES // 2, LANES), f32)
    return pl.pallas_call(
        lambda *refs: halves_kernel(*refs, phases=phases),
        out_shape=(half, half),
        in_specs=[IN_VMEM, IN_VMEM],
        out_specs=(IN_VMEM, IN_VMEM),
        compiler_params=SMALL,
        cost_estimate=pl.CostEstimate(flops=2**32, bytes_accessed=2**20, transcendentals=0),
        name="halves",
    )(kept, got)


def woven(straight, mine, got):
    groups = LANES // 2
    low = iota(mine.shape, 1) < groups
    zero, one = jnp.where(straight, mine, got), jnp.where(straight, got, mine)
    return jnp.where(low, zero, pltpu.roll(one, groups, 1)), jnp.where(low, pltpu.roll(zero, groups, 1), one)


def scale_kernel(mine_ref, got_ref, even_ref, odd_ref, mine_scale, got_scale, *, phases, devices):
    groups = LANES // 2
    per = L // phases
    half = per // 2
    tiles = phases // 4
    me = lax.axis_index("win")
    first = me % 2 == 0
    straight = panel_of(me, devices) == 0
    place = iota((LANES, LANES), 0)
    wanted = (place // (2 * phases)) * phases + place % (2 * phases) - phases
    gather = (
        ((place % (2 * phases) >= phases) & (iota((LANES, LANES), 1) % groups == wanted)).astype(f32).astype(bf16)
    )
    low = iota((half, LANES), 1) < groups
    sides = []
    for ref in (mine_ref, got_ref):
        extra = ref[groups:]
        norm = math.sqrt(CT * L) * lax.rsqrt(pick(extra, gather))[:1]
        scale = lax.rsqrt(extra + epsilon)
        scales = []
        for tile in range(2 * tiles):
            columns = []
            for phase in (2 * tile, 2 * tile + 1):
                if half >= 8:
                    count = half // 8
                    pieces = [scale[:, 2 * phases * k + phase :][:, :1] for k in range(2 * count)]
                    columns.append(
                        jnp.concatenate(
                            [jnp.where(first, pieces[k], pieces[k + count]) for k in range(count)], axis=0
                        )
                    )
                else:
                    columns.append(
                        jnp.where(first, scale[:half, phase : phase + 1], scale[half : 2 * half, phase : phase + 1])
                    )
            scales.append(jnp.where(low, columns[0], columns[1]) * norm)
        sides.append(scales)
    for tile in range(tiles):
        rows = slice(tile * half, (tile + 1) * half)
        mine_scale[rows] = sides[0][tiles + tile]
        got_scale[rows] = sides[1][tiles + tile]
        even_ref[rows], odd_ref[rows] = woven(
            straight, mine_ref[rows] * sides[0][tile], got_ref[rows] * sides[1][tile]
        )


def scaled(mine, got, phases, devices):
    half = jax.ShapeDtypeStruct((LANES // 2, LANES), f32)
    return pl.pallas_call(
        lambda *refs: scale_kernel(*refs, phases=phases, devices=devices),
        out_shape=(half,) * 4,
        in_specs=[IN_VMEM, IN_VMEM],
        out_specs=(IN_VMEM,) * 4,
        compiler_params=SMALL,
        cost_estimate=pl.CostEstimate(flops=2**32, bytes_accessed=2**18, transcendentals=0),
        name="scale",
    )(mine, got)


def finish_kernel(even_ref, odd_ref, mine_scale, got_scale, mine_ref, got_ref, out_ref, *, phases, devices):
    half = L // phases // 2
    tiles = phases // 4
    straight = panel_of(lax.axis_index("win"), devices) == 0
    mine = mine_ref[...] * mine_scale[...]
    got = got_ref[...] * got_scale[...]
    even, odd = woven(straight, mine, got)
    for tile in range(tiles):
        rows = slice(tile * half, (tile + 1) * half)
        for phase, value in enumerate((even_ref[rows], odd_ref[rows])):
            out_ref[pl.ds(2 * tile + phase, half, stride=phases), :] = value
        for phase, value in enumerate((even[rows], odd[rows])):
            out_ref[pl.ds(2 * (tiles + tile) + phase, half, stride=phases), :] = value


def finish(first, second, phases, devices):
    return pl.pallas_call(
        lambda *refs: finish_kernel(*refs, phases=phases, devices=devices),
        out_shape=jax.ShapeDtypeStruct((L // 2, LANES), f32),
        in_specs=[IN_VMEM] * 6,
        out_specs=IN_VMEM,
        compiler_params=SMALL,
        cost_estimate=pl.CostEstimate(flops=2**18, bytes_accessed=2**18, transcendentals=0),
        name="finish",
    )(*first, *second)


def masks_kernel(start_hbm, routed_ref, start_ref, sem, *, devices):
    copy = pltpu.make_async_copy(start_hbm, start_ref, sem)
    copy.start()
    held = routed_ref.shape[1]
    me = lax.axis_index("win")
    mine = panel_of(me, devices)
    per_chip = 2 * CT // devices
    row = iota((CT, held), 0)
    panels = (1 - mine, mine)
    channels = []
    for panel in panels:
        target = jnp.bitwise_xor(target_of(row // per_chip, panel, devices), me // 2)
        core = jnp.bitwise_xor(panel, panel_of(2 * target, devices))
        channel = target * per_chip + (row % per_chip + per_chip // 2 * core) % per_chip
        channels.append(channel - me * held - iota((CT, held), 1))
    copy.wait()
    for i, panel in enumerate(panels):
        routed_ref[i * CT : (i + 1) * CT] = (channels[i] + start_ref[panel] == 0).astype(f32).astype(bf16)


def masks(panel_start, held, devices):
    return pl.pallas_call(
        lambda *refs: masks_kernel(*refs, devices=devices),
        out_shape=jax.ShapeDtypeStruct((2 * CT, held), bf16),
        in_specs=[pl.BlockSpec(memory_space=pltpu.HBM)],
        out_specs=IN_VMEM,
        scratch_shapes=[pltpu.SMEM(panel_start.shape, jnp.int32), pltpu.SemaphoreType.DMA],
        compiler_params=SMALL,
        cost_estimate=pl.CostEstimate(flops=2**31, bytes_accessed=2**16, transcendentals=0),
        name="masks",
    )(panel_start)


def select_kernel(records_ref, routed_ref, *refs, begin):
    away_ref, home_ref = refs[-2:]
    both = dot(routed_ref[...], records_ref[:, begin : begin + away_ref.shape[1]]).astype(bf16)
    away_ref[...] = both[:CT]
    home_ref[...] = both[CT:]


def selected(records, routed, begin, end, *before):
    out = jax.ShapeDtypeStruct((CT, end - begin), bf16)
    return pl.pallas_call(
        lambda *refs: select_kernel(*refs, begin=begin),
        out_shape=(out, out),
        in_specs=[IN_VMEM, IN_VMEM] + [pl.BlockSpec(memory_space=pl.ANY)] * len(before),
        out_specs=(IN_VMEM, IN_VMEM),
        compiler_params=pltpu.CompilerParams(vmem_limit_bytes=SPARE),
        cost_estimate=pl.CostEstimate(flops=2**27, bytes_accessed=2**21, transcendentals=0),
        name="select",
    )(records, routed, *before)


def add_kernel(kept_ref, got_ref, *refs):
    keep_ref, send_ref = refs[-2:]
    half = keep_ref.shape[0]
    keep_ref[...] = kept_ref[:half] + got_ref[:half]
    send_ref[...] = kept_ref[half:] + got_ref[half:]


def added(kept, got, *before):
    half = kept.shape[0] // 2
    if kept.dtype == bf16 and half % 16:
        whole = kept + got
        return whole[:half], whole[half:]
    part = jax.ShapeDtypeStruct((half, *kept.shape[1:]), kept.dtype)
    return pl.pallas_call(
        add_kernel,
        out_shape=(part, part),
        in_specs=[IN_VMEM, IN_VMEM] + [pl.BlockSpec(memory_space=pl.ANY)] * len(before),
        out_specs=(IN_VMEM, IN_VMEM),
        compiler_params=SMALL,
        cost_estimate=pl.CostEstimate(flops=2**32, bytes_accessed=2**20, transcendentals=0),
        name="add",
    )(kept, got, *before)


def local(records, templates, panel_start):
    devices = lax.axis_size("win")
    panel = panel_of(lax.axis_index("win"), devices)
    phases = devices // 2
    pairs = (L // phases + 2) // 2
    orders = bits_of(devices)
    steps = len(orders[0])

    def sibling(value):
        return lax.ppermute(value, "win", [(d, d ^ 1) for d in range(devices)])

    def exchange(value, step):
        return lax.ppermute(value, "win", [(d, d ^ 1 ^ orders[panel_of(d, devices)][step]) for d in range(devices)])

    def scattered(keep, send, until, before=()):
        for step in range(until - 1):
            keep, send = added(keep, exchange(send, step), *(before if step == 0 else ()))
        return keep, exchange(send, until - 1)

    half = records.shape[1] // 2
    routed = masks(panel_start, records.shape[0], devices)
    away_late, home_late = selected(records, routed, half, 2 * half)
    got_late = sibling(away_late)
    away_early, home_early = selected(records, routed, 0, half, away_late)
    got_early = sibling(away_early)

    templates = templates.reshape(templates.shape[0], -1, L)
    other = sibling(given(templates, away_early, devices))
    late = added(home_late, got_late)
    early = added(home_early, got_early, late[0])
    w, norm = shifted(templates, other, phases, pairs, early[0])
    held = late, early
    for step in range(steps - 1):
        if step == 0:
            late_energy, squares = energy_of(held[0], [], norm, phases)
        late = added(late[0], exchange(late[1], step), *([late_energy] if step == 0 else []))
        if step == 0:
            early_energy, _ = energy_of(held[1], [squares], late[0], phases)
        early = added(early[0], exchange(early[1], step), *([early_energy] if step == 0 else []))
    late, early = [(keep, exchange(send, steps - 1)) for keep, send in (late, early)]
    rest_rows, rest_acc = correlate_late(late, w, phases)
    energy = early_energy, late_energy
    send_a, keep_a, slide = correlate_early(early, w, norm, energy, (rest_rows, rest_acc), phases, devices)
    send_b, keep_b = correlate_rest(slide, w, rest_acc, half // phases, phases, devices)

    mine, other = halves(*scattered(keep_a, send_a, steps, [send_b]), phases)
    first = scaled(mine, sibling(other), phases, devices)
    mine, other = halves(*scattered(keep_b, send_b, steps), phases)
    return finish(first, (mine, sibling(other)), phases, devices)


def solution(mesh):
    placed = (P("win", "parts"), P(None, None, "win", None), P("parts"))
    return jax.shard_map(
        local, mesh=mesh, in_specs=placed, out_specs=P(("parts", "win"), None), check_vma=False
    )
```

```python
import math

import jax
import jax.numpy as jnp
from jax import lax
from jax.experimental import pallas as pl
from jax.experimental.pallas import tpu as pltpu
from jax.sharding import PartitionSpec as P

CT = 128
L = 512
LANES = 128
epsilon = 1e-06
f32 = jnp.float32
bf16 = jnp.bfloat16
SPARE = 12 * 2**20
IN_VMEM = pl.BlockSpec(memory_space=pltpu.VMEM)
SMALL = pltpu.CompilerParams(vmem_limit_bytes=8 * 2**20)


def iota(shape, dim):
    return lax.broadcasted_iota(jnp.int32, shape, dim)


def dot(a, b, dims=(((1,), (0,)), ((), ()))):
    return lax.dot_general(a, b, dims, preferred_element_type=f32)


def split3(v):
    high = v.astype(bf16)
    rest = v - high.astype(f32)
    middle = rest.astype(bf16)
    return high, middle, (rest - middle.astype(f32)).astype(bf16)


def pick(v, m):
    return sum(dot(part, m) for part in split3(v))


def picked(m, v):
    return sum(dot(m, part) for part in split3(v))


def give_kernel(templates_hbm, before, out_ref, sem, *, devices):
    panel = panel_of(lax.axis_index("win"), devices)
    copy = pltpu.make_async_copy(templates_hbm.at[1 - panel], out_ref, sem)
    copy.start()
    copy.wait()


def given(templates, before, devices):
    return pl.pallas_call(
        lambda *refs: give_kernel(*refs, devices=devices),
        out_shape=jax.ShapeDtypeStruct(templates.shape[1:], bf16),
        in_specs=[pl.BlockSpec(memory_space=pltpu.HBM), pl.BlockSpec(memory_space=pl.ANY)],
        out_specs=IN_VMEM,
        scratch_shapes=[pltpu.SemaphoreType.DMA],
        compiler_params=SMALL,
        cost_estimate=pl.CostEstimate(flops=2**28, bytes_accessed=2**20, transcendentals=0),
        name="give",
    )(templates, before)


def shift_kernel(templates_ref, other_ref, *refs, phases, devices):
    w_ref, norm_ref, rows_ref = refs[-3:]
    gc = other_ref.shape[0]
    panel = panel_of(lax.axis_index("win"), devices)
    groups = LANES // 2
    each = gc // groups
    channels = 2 * each
    versions, total, _ = w_ref.shape
    pad = channels * phases
    front = rows_ref.shape[0] - total
    rows_ref[pl.ds(0, front + pad), :] = jnp.zeros((front + pad, LANES), f32)
    rows_ref[pl.ds(front + pad + L * channels, total - pad - L * channels), :] = jnp.zeros(
        (total - pad - L * channels, LANES), f32
    )
    norm = jnp.zeros((1, LANES), f32)
    width = min(2, each) * LANES
    lane = iota((gc, width), 1)
    offset = iota((gc, width), 0) - lane % groups * each - lane // LANES
    for side, ref in enumerate((templates_ref.at[panel], other_ref)):
        for c in range(0, each, width // LANES):
            choose = (offset == c).astype(f32).astype(bf16)
            piece = dot(ref[...], choose, (((0,), (0,)), ((), ())))
            for i in range(width // LANES):
                one = piece[:, i * LANES : (i + 1) * LANES]
                norm = norm + jnp.sum(one * one, axis=0, keepdims=True)
                rows_ref[pl.ds(front + pad + side * each + c + i, L, stride=channels), :] = one
    norm_ref[...] = jnp.broadcast_to(norm, norm_ref.shape)
    low = iota((256, LANES), 1) < groups
    for v in range(versions):
        for at in range(0, total, 256):
            size = min(256, total - at)
            start = front + at - 2 * channels * v
            even = rows_ref[pl.ds(start, size), :]
            odd = rows_ref[pl.ds(start - channels, size), :]
            w_ref[v, at : at + size, :] = jnp.where(low[:size], even, odd).astype(bf16)


def shifted(templates, other, phases, pairs, *before):
    gc = other.shape[0]
    channels = 2 * gc // 64
    versions = max(1, 8 // channels)
    total = 256 * pairs + channels * phases
    front = (2 * versions - 1) * channels + 8
    front = (front + 7) // 8 * 8
    return pl.pallas_call(
        lambda *refs: shift_kernel(*refs, phases=phases, devices=2 * phases),
        in_specs=[IN_VMEM, IN_VMEM] + [pl.BlockSpec(memory_space=pl.ANY)] * len(before),
        out_specs=(IN_VMEM, IN_VMEM),
        out_shape=(
            jax.ShapeDtypeStruct((versions, total, LANES), bf16),
            jax.ShapeDtypeStruct((8, LANES), f32),
        ),
        scratch_shapes=[pltpu.VMEM((front + total, LANES), f32)],
        compiler_params=pltpu.CompilerParams(vmem_limit_bytes=512 * (front + total) + SPARE),
        cost_estimate=pl.CostEstimate(flops=2**28, bytes_accessed=2**20, transcendentals=0),
        name="shift_templates",
    )(templates, other, *before)


def bits_of(devices):
    x, z, *rest = [1 << i for i in range(1, devices.bit_length() - 1)]
    return [x, z] + rest, [z, x] + rest


def panel_of(device, devices):
    return sum(device >> i & 1 for i in range(devices.bit_length() - 1)) % 2


def target_of(slot, panel, devices):
    mine, theirs = bits_of(devices)
    chip = jnp.zeros_like(slot)
    for i, (p, q) in enumerate(zip(mine, theirs)):
        chip += (slot >> (len(mine) - 1 - i) & 1) * jnp.where(panel == 0, p, q)
    return chip // 2


def spread(value, repeat, spread_ref, phases):
    t = value.shape[1]
    spread_ref[...] = dot(value, repeat, (((0,), (0,)), ((), ())))
    count = t // phases
    phase = iota((count, LANES), 1) // (LANES // phases)
    rows = jnp.zeros((count, LANES), f32)
    for k in range(phases):
        rows = jnp.where(phase == k, spread_ref[pl.ds(k, count, stride=phases), :], rows)
    return rows


def spread_pieces(pieces, spread_ref, phases):
    value = sum(r[...] for r in pieces[1:]) + pieces[0][...]
    channels = value.shape[0]
    repeat = (iota((channels, LANES), 0) == iota((channels, LANES), 1) % channels).astype(f32).astype(bf16)
    return spread(value, repeat, spread_ref, phases)


def fill_slide(rows_ref, slide_ref):
    span = slide_ref.shape[1]
    for k in range(slide_ref.shape[0]):
        slide_ref[k, :, 0:LANES] = rows_ref[pl.ds(2 * k, span), :].astype(bf16)
        slide_ref[k, :, LANES:] = rows_ref[pl.ds(2 * k + 1, span), :].astype(bf16)


def energies(squares, m, phases):
    n = squares.shape[0]
    channels = LANES // phases
    per = L // phases
    left, right = iota((LANES, LANES), 0) // channels, iota((LANES, LANES), 1) % (2 * phases)
    inside = right < phases
    tail = (inside & (left >= right)).astype(f32).astype(bf16)
    head = (inside & (left < right)).astype(f32).astype(bf16)
    sums = jnp.broadcast_to(jnp.sum(squares, axis=1, keepdims=True), squares.shape)
    distance = iota((m, n), 1) - iota((m, n), 0)
    band = ((distance >= 1) & (distance < per)).astype(f32).astype(bf16)
    begin = pick(squares[per : min(n, per + m)], head)
    if per + m > n:
        begin = jnp.concatenate([begin, jnp.zeros((per + m - n, LANES), f32)], axis=0)
    return pick(squares[:m], tail) + picked(band, sums) + begin


def energy_kernel(first_ref, second_ref, *refs, phases):
    out_ref, squares_ref, spread_ref = refs[-3:]
    squares = jnp.zeros((1, first_ref.shape[1]), f32)
    for ref in (first_ref, second_ref):
        value = ref[...].astype(f32)
        squares = squares + jnp.sum(value * value, axis=0, keepdims=True)
    parts = list(split3(squares)) + [jnp.zeros((13, squares.shape[1]), bf16)]
    repeat = ((iota((16, LANES), 1) % (LANES // phases) == 0) & (iota((16, LANES), 0) < 3)).astype(f32).astype(bf16)
    rows = spread(jnp.concatenate(parts, axis=0), repeat, spread_ref, phases)
    squares_ref[...] = rows
    following = [ref[...] for ref in refs[:-4]]
    out_ref[...] = energies(jnp.concatenate([rows] + following, axis=0), rows.shape[0], phases)


def energy_of(chunk, following, before, phases):
    t = chunk[0].shape[1]
    shapes = [pltpu.VMEM((t, LANES), f32)]
    out = jax.ShapeDtypeStruct((t // phases, LANES), f32)
    return pl.pallas_call(
        lambda *refs: energy_kernel(*refs, phases=phases),
        out_shape=(out, out),
        in_specs=[IN_VMEM] * (2 + len(following)) + [pl.BlockSpec(memory_space=pl.ANY)],
        out_specs=(IN_VMEM, IN_VMEM),
        scratch_shapes=shapes,
        compiler_params=grant(shapes),
        cost_estimate=pl.CostEstimate(flops=2**28, bytes_accessed=2**20, transcendentals=0),
        name="energy",
    )(*chunk, *following, before)


def correlate_tiles(slides, w_ref, acc_ref, tiles, phases):
    versions = w_ref.shape[0]
    channels = LANES // phases
    pairs = (w_ref.shape[1] - LANES) // 256
    m = sum(count for _, count in slides)

    def shifts(q, tile):
        v = tile % versions
        return w_ref[v, pl.ds(LANES + 256 * q - 2 * channels * (tile - v), 256), :]

    for q in range(pairs):
        window = [slide[q % 8, pl.ds(16 * (q // 8), count), :] for slide, count in slides]
        window = window[0] if len(window) == 1 else jnp.concatenate(window, axis=0)
        term = dot(window, jnp.concatenate([shifts(q, tile) for tile in tiles], axis=1))
        if q == 0:
            acc_ref[pl.ds(0, m), :] = term
        else:
            acc_ref[pl.ds(0, m), :] += term


def late_kernel(*refs, phases):
    *pieces, w_ref, out_rows, out_acc, spread_ref, rows_ref, slide_ref = refs
    rows = spread_pieces(pieces, spread_ref, phases)
    count = rows.shape[0]
    out_rows[...] = rows
    rows_ref[pl.ds(0, count), :] = rows
    rows_ref[pl.ds(count, rows_ref.shape[0] - count), :] = jnp.zeros((rows_ref.shape[0] - count, LANES), f32)
    fill_slide(rows_ref, slide_ref)
    correlate_tiles([(slide_ref, count)], w_ref, out_acc, range(phases // 2), phases)


def write_blocks(send_ref, keep_ref, acc_ref, lead, per, devices):
    me = lax.axis_index("win")
    kept = keep_ref.shape[0]
    for slot in range(2 * kept):
        chip = jnp.bitwise_xor(me // 2, target_of(jnp.int32(slot), panel_of(me, devices), devices))
        at = pl.multiple_of(chip * per, 8)
        ref = keep_ref if slot < kept else send_ref
        for tile in range(acc_ref.shape[1] // LANES):
            ref[slot % kept, tile * per : (tile + 1) * per, :] = acc_ref[
                pl.ds(at, per), tile * LANES : (tile + 1) * LANES
            ]
        if lead is not None:
            ref[slot % kept, LANES:, :] = lead(at)


def early_kernel(*refs, phases, devices):
    *pieces, w_ref, norm_ref, early_energy, late_energy, rest_rows, rest_acc = refs[: len(refs) - 7]
    send_ref, keep_ref, slide_ref, rows_ref, spread_ref, energy_ref, acc_ref = refs[len(refs) - 7 :]
    rows = spread_pieces(pieces, spread_ref, phases)
    m = rows.shape[0]
    n = m + rest_rows.shape[0]
    rows_ref[pl.ds(0, m), :] = rows
    rows_ref[pl.ds(m, n - m), :] = rest_rows[...]
    fill_slide(rows_ref, slide_ref)
    acc_ref[pl.ds(m, n - m), :] = rest_acc[:, : acc_ref.shape[1]]
    correlate_tiles([(slide_ref, m)], w_ref, acc_ref, range(phases // 4), phases)

    energy_ref[pl.ds(0, m), :] = early_energy[...]
    energy_ref[pl.ds(m, n - m), :] = late_energy[...]
    per = L // phases
    place = iota((LANES, LANES), 1)
    wanted = (place // (2 * phases)) * phases + place % (2 * phases) - phases
    scatter = ((place % (2 * phases) >= phases) & (iota((LANES, LANES), 0) == wanted)).astype(f32).astype(bf16)
    norm = pick(norm_ref[...], scatter)
    lane = iota((8, LANES), 1)

    def extras(at):
        e = norm
        for k in range(per // 8):
            e = jnp.where(
                (lane // (2 * phases) == k) & (lane % (2 * phases) < phases), energy_ref[pl.ds(at + 8 * k, 8), :], e
            )
        return e

    write_blocks(send_ref, keep_ref, acc_ref, extras, per, devices)


def rest_kernel(slide_ref, w_ref, rest_acc, send_ref, keep_ref, acc_ref, *, phases, devices):
    n, width = acc_ref.shape
    m = n - rest_acc.shape[0]
    acc_ref[pl.ds(m, n - m), :] = rest_acc[:, width:]
    correlate_tiles([(slide_ref, m)], w_ref, acc_ref, range(phases // 4, phases // 2), phases)
    write_blocks(send_ref, keep_ref, acc_ref, None, L // phases, devices)


def grant(shapes):
    return pltpu.CompilerParams(vmem_limit_bytes=sum(math.prod(s.shape) * 4 for s in shapes) + SPARE)


def slide_shape(m, phases):
    pairs = (L // phases + 2) // 2
    return (min(8, pairs), m + 16 * ((pairs - 1) // 8), 256)


def correlate_late(pieces, w, phases):
    t = pieces[0].shape[1]
    count = t // phases
    slide = slide_shape(count, phases)
    shapes = [pltpu.VMEM((t, LANES), f32), pltpu.VMEM((slide[1] + 16, LANES), f32), pltpu.VMEM(slide, bf16)]
    return pl.pallas_call(
        lambda *refs: late_kernel(*refs, phases=phases),
        out_shape=(
            jax.ShapeDtypeStruct((count, LANES), f32),
            jax.ShapeDtypeStruct((count, phases * 64), f32),
        ),
        in_specs=[IN_VMEM] * (len(pieces) + 1),
        out_specs=(IN_VMEM,) * 2,
        scratch_shapes=shapes,
        compiler_params=grant(shapes),
        cost_estimate=pl.CostEstimate(flops=2**31, bytes_accessed=2**22, transcendentals=0),
        name="correlate_late",
    )(*pieces, w)


def correlate_early(pieces, w, norm, energy, rest, phases, devices):
    t = pieces[0].shape[1]
    m = t // phases
    n = m + rest[0].shape[0]
    shapes = [
        pltpu.VMEM((n, LANES), f32),
        pltpu.VMEM((t, LANES), f32),
        pltpu.VMEM((n, LANES), f32),
        pltpu.VMEM((n, phases * 32), f32),
    ]
    block = jax.ShapeDtypeStruct((devices // 4, LANES + 8, LANES), f32)
    return pl.pallas_call(
        lambda *refs: early_kernel(*refs, phases=phases, devices=devices),
        out_shape=(block, block, jax.ShapeDtypeStruct(slide_shape(m, phases), bf16)),
        in_specs=[IN_VMEM] * (len(pieces) + 6),
        out_specs=(IN_VMEM,) * 3,
        scratch_shapes=shapes,
        compiler_params=grant(shapes),
        cost_estimate=pl.CostEstimate(flops=2**32, bytes_accessed=2**24, transcendentals=0),
        name="correlate_early",
    )(*pieces, w, norm, *energy, *rest)


def correlate_rest(slide, w, rest_acc, m, phases, devices):
    shapes = [pltpu.VMEM((m + rest_acc.shape[0], phases * 32), f32)]
    block = jax.ShapeDtypeStruct((devices // 4, LANES, LANES), f32)
    return pl.pallas_call(
        lambda *refs: rest_kernel(*refs, phases=phases, devices=devices),
        out_shape=(block, block),
        in_specs=[IN_VMEM] * 3,
        out_specs=(IN_VMEM, IN_VMEM),
        scratch_shapes=shapes,
        compiler_params=grant(shapes),
        cost_estimate=pl.CostEstimate(flops=2**33, bytes_accessed=2**24, transcendentals=0),
        name="correlate_rest",
    )(slide, w, rest_acc)


def cut(block, phases):
    per = L // phases
    half = per // 2
    starts = range(0, LANES, per)
    return (
        jnp.concatenate([block[at : at + half] for at in starts], axis=0),
        jnp.concatenate([block[at + half : at + per] for at in starts], axis=0),
    )


def halves_kernel(kept_ref, got_ref, mine_ref, other_ref, *, phases):
    first = lax.axis_index("win") % 2 == 0
    block = kept_ref[0] + got_ref[0]
    lower, upper = cut(block, phases)
    rows = LANES // 2
    mine_ref[0:rows] = jnp.where(first, lower, upper)
    other_ref[0:rows] = jnp.where(first, upper, lower)
    if block.shape[0] > LANES:
        mine_ref[rows:] = block[LANES:]
        other_ref[rows:] = block[LANES:]


def halves(kept, got, phases):
    half = jax.ShapeDtypeStruct((kept.shape[1] - LANES // 2, LANES), f32)
    return pl.pallas_call(
        lambda *refs: halves_kernel(*refs, phases=phases),
        out_shape=(half, half),
        in_specs=[IN_VMEM, IN_VMEM],
        out_specs=(IN_VMEM, IN_VMEM),
        compiler_params=SMALL,
        cost_estimate=pl.CostEstimate(flops=2**32, bytes_accessed=2**20, transcendentals=0),
        name="halves",
    )(kept, got)


def woven(straight, mine, got):
    groups = LANES // 2
    low = iota(mine.shape, 1) < groups
    zero, one = jnp.where(straight, mine, got), jnp.where(straight, got, mine)
    return jnp.where(low, zero, pltpu.roll(one, groups, 1)), jnp.where(low, pltpu.roll(zero, groups, 1), one)


def scale_kernel(mine_ref, got_ref, even_ref, odd_ref, mine_scale, got_scale, *, phases, devices):
    groups = LANES // 2
    per = L // phases
    half = per // 2
    tiles = phases // 4
    me = lax.axis_index("win")
    first = me % 2 == 0
    straight = panel_of(me, devices) == 0
    place = iota((LANES, LANES), 0)
    wanted = (place // (2 * phases)) * phases + place % (2 * phases) - phases
    gather = (
        ((place % (2 * phases) >= phases) & (iota((LANES, LANES), 1) % groups == wanted)).astype(f32).astype(bf16)
    )
    low = iota((half, LANES), 1) < groups
    sides = []
    for ref in (mine_ref, got_ref):
        extra = ref[groups:]
        norm = math.sqrt(CT * L) * lax.rsqrt(pick(extra, gather))[:1]
        scale = lax.rsqrt(extra + epsilon)
        scales = []
        for tile in range(2 * tiles):
            columns = []
            for phase in (2 * tile, 2 * tile + 1):
                if half >= 8:
                    count = half // 8
                    pieces = [scale[:, 2 * phases * k + phase :][:, :1] for k in range(2 * count)]
                    columns.append(
                        jnp.concatenate(
                            [jnp.where(first, pieces[k], pieces[k + count]) for k in range(count)], axis=0
                        )
                    )
                else:
                    columns.append(
                        jnp.where(first, scale[:half, phase : phase + 1], scale[half : 2 * half, phase : phase + 1])
                    )
            scales.append(jnp.where(low, columns[0], columns[1]) * norm)
        sides.append(scales)
    for tile in range(tiles):
        rows = slice(tile * half, (tile + 1) * half)
        mine_scale[rows] = sides[0][tiles + tile]
        got_scale[rows] = sides[1][tiles + tile]
        even_ref[rows], odd_ref[rows] = woven(
            straight, mine_ref[rows] * sides[0][tile], got_ref[rows] * sides[1][tile]
        )


def scaled(mine, got, phases, devices):
    half = jax.ShapeDtypeStruct((LANES // 2, LANES), f32)
    return pl.pallas_call(
        lambda *refs: scale_kernel(*refs, phases=phases, devices=devices),
        out_shape=(half,) * 4,
        in_specs=[IN_VMEM, IN_VMEM],
        out_specs=(IN_VMEM,) * 4,
        compiler_params=SMALL,
        cost_estimate=pl.CostEstimate(flops=2**32, bytes_accessed=2**18, transcendentals=0),
        name="scale",
    )(mine, got)


def finish_kernel(even_ref, odd_ref, mine_scale, got_scale, mine_ref, got_ref, out_ref, *, phases, devices):
    half = L // phases // 2
    tiles = phases // 4
    straight = panel_of(lax.axis_index("win"), devices) == 0
    mine = mine_ref[...] * mine_scale[...]
    got = got_ref[...] * got_scale[...]
    even, odd = woven(straight, mine, got)
    for tile in range(tiles):
        rows = slice(tile * half, (tile + 1) * half)
        for phase, value in enumerate((even_ref[rows], odd_ref[rows])):
            out_ref[pl.ds(2 * tile + phase, half, stride=phases), :] = value
        for phase, value in enumerate((even[rows], odd[rows])):
            out_ref[pl.ds(2 * (tiles + tile) + phase, half, stride=phases), :] = value


def finish(first, second, phases, devices):
    return pl.pallas_call(
        lambda *refs: finish_kernel(*refs, phases=phases, devices=devices),
        out_shape=jax.ShapeDtypeStruct((L // 2, LANES), f32),
        in_specs=[IN_VMEM] * 6,
        out_specs=IN_VMEM,
        compiler_params=SMALL,
        cost_estimate=pl.CostEstimate(flops=2**18, bytes_accessed=2**18, transcendentals=0),
        name="finish",
    )(*first, *second)


def masks_kernel(start_hbm, routed_ref, start_ref, sem, *, devices):
    copy = pltpu.make_async_copy(start_hbm, start_ref, sem)
    copy.start()
    held = routed_ref.shape[1]
    me = lax.axis_index("win")
    mine = panel_of(me, devices)
    per_chip = 2 * CT // devices
    row = iota((CT, held), 0)
    panels = (1 - mine, mine)
    channels = []
    for panel in panels:
        target = jnp.bitwise_xor(target_of(row // per_chip, panel, devices), me // 2)
        core = jnp.bitwise_xor(panel, panel_of(2 * target, devices))
        channel = target * per_chip + (row % per_chip + per_chip // 2 * core) % per_chip
        channels.append(channel - me * held - iota((CT, held), 1))
    copy.wait()
    for i, panel in enumerate(panels):
        routed_ref[i * CT : (i + 1) * CT] = (channels[i] + start_ref[panel] == 0).astype(f32).astype(bf16)


def masks(panel_start, held, devices):
    return pl.pallas_call(
        lambda *refs: masks_kernel(*refs, devices=devices),
        out_shape=jax.ShapeDtypeStruct((2 * CT, held), bf16),
        in_specs=[pl.BlockSpec(memory_space=pltpu.HBM)],
        out_specs=IN_VMEM,
        scratch_shapes=[pltpu.SMEM(panel_start.shape, jnp.int32), pltpu.SemaphoreType.DMA],
        compiler_params=SMALL,
        cost_estimate=pl.CostEstimate(flops=2**31, bytes_accessed=2**16, transcendentals=0),
        name="masks",
    )(panel_start)


def select_kernel(records_ref, routed_ref, *refs, begin):
    away_ref, home_ref = refs[-2:]
    both = dot(routed_ref[...], records_ref[:, begin : begin + away_ref.shape[1]]).astype(bf16)
    away_ref[...] = both[:CT]
    home_ref[...] = both[CT:]


def selected(records, routed, begin, end, *before):
    out = jax.ShapeDtypeStruct((CT, end - begin), bf16)
    return pl.pallas_call(
        lambda *refs: select_kernel(*refs, begin=begin),
        out_shape=(out, out),
        in_specs=[IN_VMEM, IN_VMEM] + [pl.BlockSpec(memory_space=pl.ANY)] * len(before),
        out_specs=(IN_VMEM, IN_VMEM),
        compiler_params=pltpu.CompilerParams(vmem_limit_bytes=SPARE),
        cost_estimate=pl.CostEstimate(flops=2**27, bytes_accessed=2**21, transcendentals=0),
        name="select",
    )(records, routed, *before)


def add_kernel(kept_ref, got_ref, *refs):
    keep_ref, send_ref = refs[-2:]
    half = keep_ref.shape[0]
    keep_ref[...] = kept_ref[:half] + got_ref[:half]
    send_ref[...] = kept_ref[half:] + got_ref[half:]


def added(kept, got, *before):
    half = kept.shape[0] // 2
    if kept.dtype == bf16 and half % 16:
        whole = kept + got
        return whole[:half], whole[half:]
    part = jax.ShapeDtypeStruct((half, *kept.shape[1:]), kept.dtype)
    return pl.pallas_call(
        add_kernel,
        out_shape=(part, part),
        in_specs=[IN_VMEM, IN_VMEM] + [pl.BlockSpec(memory_space=pl.ANY)] * len(before),
        out_specs=(IN_VMEM, IN_VMEM),
        compiler_params=SMALL,
        cost_estimate=pl.CostEstimate(flops=2**32, bytes_accessed=2**20, transcendentals=0),
        name="add",
    )(kept, got, *before)


def local(records, templates, panel_start):
    devices = lax.axis_size("win")
    panel = panel_of(lax.axis_index("win"), devices)
    phases = devices // 2
    pairs = (L // phases + 2) // 2
    orders = bits_of(devices)
    steps = len(orders[0])

    def sibling(value):
        return lax.ppermute(value, "win", [(d, d ^ 1) for d in range(devices)])

    def exchange(value, step):
        return lax.ppermute(value, "win", [(d, d ^ 1 ^ orders[panel_of(d, devices)][step]) for d in range(devices)])

    def scattered(keep, send, until, before=()):
        for step in range(until - 1):
            keep, send = added(keep, exchange(send, step), *(before if step == 0 else ()))
        return keep, exchange(send, until - 1)

    half = records.shape[1] // 2
    routed = masks(panel_start, records.shape[0], devices)
    away_late, home_late = selected(records, routed, half, 2 * half)
    got_late = sibling(away_late)
    away_early, home_early = selected(records, routed, 0, half, away_late)
    got_early = sibling(away_early)

    templates = templates.reshape(templates.shape[0], -1, L)
    other = sibling(given(templates, away_early, devices))
    late = added(home_late, got_late)
    early = added(home_early, got_early, late[0])
    w, norm = shifted(templates, other, phases, pairs, early[0])
    held = late, early
    for step in range(steps - 1):
        if step == 0:
            late_energy, squares = energy_of(held[0], [], norm, phases)
        late = added(late[0], exchange(late[1], step), *([late_energy] if step == 0 else []))
        if step == 0:
            early_energy, _ = energy_of(held[1], [squares], late[0], phases)
        early = added(early[0], exchange(early[1], step), *([early_energy] if step == 0 else []))
    late, early = [(keep, exchange(send, steps - 1)) for keep, send in (late, early)]
    rest_rows, rest_acc = correlate_late(late, w, phases)
    energy = early_energy, late_energy
    send_a, keep_a, slide = correlate_early(early, w, norm, energy, (rest_rows, rest_acc), phases, devices)
    send_b, keep_b = correlate_rest(slide, w, rest_acc, half // phases, phases, devices)

    mine, other = halves(*scattered(keep_a, send_a, steps, [send_b]), phases)
    first = scaled(mine, sibling(other), phases, devices)
    mine, other = halves(*scattered(keep_b, send_b, steps), phases)
    return finish(first, (mine, sibling(other)), phases, devices)


def solution(mesh):
    placed = (P("win", "parts"), P(None, None, "win", None), P("parts"))
    return jax.shard_map(
        local, mesh=mesh, in_specs=placed, out_specs=P(("parts", "win"), None), check_vma=False
    )
```

```python
import math

import jax
import jax.numpy as jnp
from jax import lax
from jax.experimental import pallas as pl
from jax.experimental.pallas import tpu as pltpu
from jax.sharding import PartitionSpec as P

CT = 128
L = 512
LANES = 128
epsilon = 1e-06
f32 = jnp.float32
bf16 = jnp.bfloat16
SPARE = 12 * 2**20
IN_VMEM = pl.BlockSpec(memory_space=pltpu.VMEM)
SMALL = pltpu.CompilerParams(vmem_limit_bytes=8 * 2**20)


def iota(shape, dim):
    return lax.broadcasted_iota(jnp.int32, shape, dim)


def dot(a, b, dims=(((1,), (0,)), ((), ()))):
    return lax.dot_general(a, b, dims, preferred_element_type=f32)


def split3(v):
    high = v.astype(bf16)
    rest = v - high.astype(f32)
    middle = rest.astype(bf16)
    return high, middle, (rest - middle.astype(f32)).astype(bf16)


def pick(v, m):
    return sum(dot(part, m) for part in split3(v))


def picked(m, v):
    return sum(dot(m, part) for part in split3(v))


def give_kernel(templates_hbm, before, out_ref, sem, *, devices):
    panel = panel_of(lax.axis_index("win"), devices)
    copy = pltpu.make_async_copy(templates_hbm.at[1 - panel], out_ref, sem)
    copy.start()
    copy.wait()


def given(templates, before, devices):
    return pl.pallas_call(
        lambda *refs: give_kernel(*refs, devices=devices),
        out_shape=jax.ShapeDtypeStruct(templates.shape[1:], bf16),
        in_specs=[pl.BlockSpec(memory_space=pltpu.HBM), pl.BlockSpec(memory_space=pl.ANY)],
        out_specs=IN_VMEM,
        scratch_shapes=[pltpu.SemaphoreType.DMA],
        compiler_params=SMALL,
        cost_estimate=pl.CostEstimate(flops=2**28, bytes_accessed=2**20, transcendentals=0),
        name="give",
    )(templates, before)


def shift_kernel(templates_ref, other_ref, *refs, phases, devices):
    w_ref, norm_ref, rows_ref = refs[-3:]
    gc = other_ref.shape[0]
    panel = panel_of(lax.axis_index("win"), devices)
    groups = LANES // 2
    each = gc // groups
    channels = 2 * each
    versions, total, _ = w_ref.shape
    pad = channels * phases
    front = rows_ref.shape[0] - total
    rows_ref[pl.ds(0, front + pad), :] = jnp.zeros((front + pad, LANES), f32)
    rows_ref[pl.ds(front + pad + L * channels, total - pad - L * channels), :] = jnp.zeros(
        (total - pad - L * channels, LANES), f32
    )
    norm = jnp.zeros((1, LANES), f32)
    width = min(2, each) * LANES
    lane = iota((gc, width), 1)
    offset = iota((gc, width), 0) - lane % groups * each - lane // LANES
    for side, ref in enumerate((templates_ref.at[panel], other_ref)):
        for c in range(0, each, width // LANES):
            choose = (offset == c).astype(f32).astype(bf16)
            piece = dot(ref[...], choose, (((0,), (0,)), ((), ())))
            for i in range(width // LANES):
                one = piece[:, i * LANES : (i + 1) * LANES]
                norm = norm + jnp.sum(one * one, axis=0, keepdims=True)
                rows_ref[pl.ds(front + pad + side * each + c + i, L, stride=channels), :] = one
    norm_ref[...] = jnp.broadcast_to(norm, norm_ref.shape)
    low = iota((256, LANES), 1) < groups
    for v in range(versions):
        for at in range(0, total, 256):
            size = min(256, total - at)
            start = front + at - 2 * channels * v
            even = rows_ref[pl.ds(start, size), :]
            odd = rows_ref[pl.ds(start - channels, size), :]
            w_ref[v, at : at + size, :] = jnp.where(low[:size], even, odd).astype(bf16)


def shifted(templates, other, phases, pairs, *before):
    gc = other.shape[0]
    channels = 2 * gc // 64
    versions = max(1, 8 // channels)
    total = 256 * pairs + channels * phases
    front = (2 * versions - 1) * channels + 8
    front = (front + 7) // 8 * 8
    return pl.pallas_call(
        lambda *refs: shift_kernel(*refs, phases=phases, devices=2 * phases),
        in_specs=[IN_VMEM, IN_VMEM] + [pl.BlockSpec(memory_space=pl.ANY)] * len(before),
        out_specs=(IN_VMEM, IN_VMEM),
        out_shape=(
            jax.ShapeDtypeStruct((versions, total, LANES), bf16),
            jax.ShapeDtypeStruct((8, LANES), f32),
        ),
        scratch_shapes=[pltpu.VMEM((front + total, LANES), f32)],
        compiler_params=pltpu.CompilerParams(vmem_limit_bytes=512 * (front + total) + SPARE),
        cost_estimate=pl.CostEstimate(flops=2**28, bytes_accessed=2**20, transcendentals=0),
        name="shift_templates",
    )(templates, other, *before)


def bits_of(devices):
    x, z, *rest = [1 << i for i in range(1, devices.bit_length() - 1)]
    return [z, x] + rest, [x, z] + rest


def panel_of(device, devices):
    return sum(device >> i & 1 for i in range(devices.bit_length() - 1)) % 2


def target_of(slot, panel, devices):
    mine, theirs = bits_of(devices)
    chip = jnp.zeros_like(slot)
    for i, (p, q) in enumerate(zip(mine, theirs)):
        chip += (slot >> (len(mine) - 1 - i) & 1) * jnp.where(panel == 0, p, q)
    return chip // 2


def spread(value, repeat, spread_ref, phases):
    t = value.shape[1]
    spread_ref[...] = dot(value, repeat, (((0,), (0,)), ((), ())))
    count = t // phases
    phase = iota((count, LANES), 1) // (LANES // phases)
    rows = jnp.zeros((count, LANES), f32)
    for k in range(phases):
        rows = jnp.where(phase == k, spread_ref[pl.ds(k, count, stride=phases), :], rows)
    return rows


def spread_pieces(pieces, spread_ref, phases):
    value = sum(r[...] for r in pieces[1:]) + pieces[0][...]
    channels = value.shape[0]
    repeat = (iota((channels, LANES), 0) == iota((channels, LANES), 1) % channels).astype(f32).astype(bf16)
    return spread(value, repeat, spread_ref, phases)


def fill_slide(rows_ref, slide_ref):
    span = slide_ref.shape[1]
    for k in range(slide_ref.shape[0]):
        slide_ref[k, :, 0:LANES] = rows_ref[pl.ds(2 * k, span), :].astype(bf16)
        slide_ref[k, :, LANES:] = rows_ref[pl.ds(2 * k + 1, span), :].astype(bf16)


def energies(squares, m, phases):
    n = squares.shape[0]
    channels = LANES // phases
    per = L // phases
    left, right = iota((LANES, LANES), 0) // channels, iota((LANES, LANES), 1) % (2 * phases)
    inside = right < phases
    tail = (inside & (left >= right)).astype(f32).astype(bf16)
    head = (inside & (left < right)).astype(f32).astype(bf16)
    sums = jnp.broadcast_to(jnp.sum(squares, axis=1, keepdims=True), squares.shape)
    distance = iota((m, n), 1) - iota((m, n), 0)
    band = ((distance >= 1) & (distance < per)).astype(f32).astype(bf16)
    begin = pick(squares[per : min(n, per + m)], head)
    if per + m > n:
        begin = jnp.concatenate([begin, jnp.zeros((per + m - n, LANES), f32)], axis=0)
    return pick(squares[:m], tail) + picked(band, sums) + begin


def energy_kernel(first_ref, second_ref, *refs, phases):
    out_ref, squares_ref, spread_ref = refs[-3:]
    squares = jnp.zeros((1, first_ref.shape[1]), f32)
    for ref in (first_ref, second_ref):
        value = ref[...].astype(f32)
        squares = squares + jnp.sum(value * value, axis=0, keepdims=True)
    parts = list(split3(squares)) + [jnp.zeros((13, squares.shape[1]), bf16)]
    repeat = ((iota((16, LANES), 1) % (LANES // phases) == 0) & (iota((16, LANES), 0) < 3)).astype(f32).astype(bf16)
    rows = spread(jnp.concatenate(parts, axis=0), repeat, spread_ref, phases)
    squares_ref[...] = rows
    following = [ref[...] for ref in refs[:-4]]
    out_ref[...] = energies(jnp.concatenate([rows] + following, axis=0), rows.shape[0], phases)


def energy_of(chunk, following, before, phases):
    t = chunk[0].shape[1]
    shapes = [pltpu.VMEM((t, LANES), f32)]
    out = jax.ShapeDtypeStruct((t // phases, LANES), f32)
    return pl.pallas_call(
        lambda *refs: energy_kernel(*refs, phases=phases),
        out_shape=(out, out),
        in_specs=[IN_VMEM] * (2 + len(following)) + [pl.BlockSpec(memory_space=pl.ANY)],
        out_specs=(IN_VMEM, IN_VMEM),
        scratch_shapes=shapes,
        compiler_params=grant(shapes),
        cost_estimate=pl.CostEstimate(flops=2**28, bytes_accessed=2**20, transcendentals=0),
        name="energy",
    )(*chunk, *following, before)


def correlate_tiles(slides, w_ref, acc_ref, tiles, phases):
    versions = w_ref.shape[0]
    channels = LANES // phases
    pairs = (w_ref.shape[1] - LANES) // 256
    m = sum(count for _, count in slides)

    def shifts(q, tile):
        v = tile % versions
        return w_ref[v, pl.ds(LANES + 256 * q - 2 * channels * (tile - v), 256), :]

    for q in range(pairs):
        window = [slide[q % 8, pl.ds(16 * (q // 8), count), :] for slide, count in slides]
        window = window[0] if len(window) == 1 else jnp.concatenate(window, axis=0)
        term = dot(window, jnp.concatenate([shifts(q, tile) for tile in tiles], axis=1))
        if q == 0:
            acc_ref[pl.ds(0, m), :] = term
        else:
            acc_ref[pl.ds(0, m), :] += term


def late_kernel(*refs, phases):
    *pieces, w_ref, out_rows, out_acc, spread_ref, rows_ref, slide_ref = refs
    rows = spread_pieces(pieces, spread_ref, phases)
    count = rows.shape[0]
    out_rows[...] = rows
    rows_ref[pl.ds(0, count), :] = rows
    rows_ref[pl.ds(count, rows_ref.shape[0] - count), :] = jnp.zeros((rows_ref.shape[0] - count, LANES), f32)
    fill_slide(rows_ref, slide_ref)
    correlate_tiles([(slide_ref, count)], w_ref, out_acc, range(phases // 2), phases)


def write_blocks(send_ref, keep_ref, acc_ref, lead, per, devices):
    me = lax.axis_index("win")
    kept = keep_ref.shape[0]
    for slot in range(2 * kept):
        chip = jnp.bitwise_xor(me // 2, target_of(jnp.int32(slot), panel_of(me, devices), devices))
        at = pl.multiple_of(chip * per, 8)
        ref = keep_ref if slot < kept else send_ref
        for tile in range(acc_ref.shape[1] // LANES):
            ref[slot % kept, tile * per : (tile + 1) * per, :] = acc_ref[
                pl.ds(at, per), tile * LANES : (tile + 1) * LANES
            ]
        if lead is not None:
            ref[slot % kept, LANES:, :] = lead(at)


def early_kernel(*refs, phases, devices):
    *pieces, w_ref, norm_ref, early_energy, late_energy, rest_rows, rest_acc = refs[: len(refs) - 7]
    send_ref, keep_ref, slide_ref, rows_ref, spread_ref, energy_ref, acc_ref = refs[len(refs) - 7 :]
    rows = spread_pieces(pieces, spread_ref, phases)
    m = rows.shape[0]
    n = m + rest_rows.shape[0]
    rows_ref[pl.ds(0, m), :] = rows
    rows_ref[pl.ds(m, n - m), :] = rest_rows[...]
    fill_slide(rows_ref, slide_ref)
    acc_ref[pl.ds(m, n - m), :] = rest_acc[:, : acc_ref.shape[1]]
    correlate_tiles([(slide_ref, m)], w_ref, acc_ref, range(phases // 4), phases)

    energy_ref[pl.ds(0, m), :] = early_energy[...]
    energy_ref[pl.ds(m, n - m), :] = late_energy[...]
    per = L // phases
    place = iota((LANES, LANES), 1)
    wanted = (place // (2 * phases)) * phases + place % (2 * phases) - phases
    scatter = ((place % (2 * phases) >= phases) & (iota((LANES, LANES), 0) == wanted)).astype(f32).astype(bf16)
    norm = pick(norm_ref[...], scatter)
    lane = iota((8, LANES), 1)

    def extras(at):
        e = norm
        for k in range(per // 8):
            e = jnp.where(
                (lane // (2 * phases) == k) & (lane % (2 * phases) < phases), energy_ref[pl.ds(at + 8 * k, 8), :], e
            )
        return e

    write_blocks(send_ref, keep_ref, acc_ref, extras, per, devices)


def rest_kernel(slide_ref, w_ref, rest_acc, send_ref, keep_ref, acc_ref, *, phases, devices):
    n, width = acc_ref.shape
    m = n - rest_acc.shape[0]
    acc_ref[pl.ds(m, n - m), :] = rest_acc[:, width:]
    correlate_tiles([(slide_ref, m)], w_ref, acc_ref, range(phases // 4, phases // 2), phases)
    write_blocks(send_ref, keep_ref, acc_ref, None, L // phases, devices)


def grant(shapes):
    return pltpu.CompilerParams(vmem_limit_bytes=sum(math.prod(s.shape) * 4 for s in shapes) + SPARE)


def slide_shape(m, phases):
    pairs = (L // phases + 2) // 2
    return (min(8, pairs), m + 16 * ((pairs - 1) // 8), 256)


def correlate_late(pieces, w, phases):
    t = pieces[0].shape[1]
    count = t // phases
    slide = slide_shape(count, phases)
    shapes = [pltpu.VMEM((t, LANES), f32), pltpu.VMEM((slide[1] + 16, LANES), f32), pltpu.VMEM(slide, bf16)]
    return pl.pallas_call(
        lambda *refs: late_kernel(*refs, phases=phases),
        out_shape=(
            jax.ShapeDtypeStruct((count, LANES), f32),
            jax.ShapeDtypeStruct((count, phases * 64), f32),
        ),
        in_specs=[IN_VMEM] * (len(pieces) + 1),
        out_specs=(IN_VMEM,) * 2,
        scratch_shapes=shapes,
        compiler_params=grant(shapes),
        cost_estimate=pl.CostEstimate(flops=2**31, bytes_accessed=2**22, transcendentals=0),
        name="correlate_late",
    )(*pieces, w)


def correlate_early(pieces, w, norm, energy, rest, phases, devices):
    t = pieces[0].shape[1]
    m = t // phases
    n = m + rest[0].shape[0]
    shapes = [
        pltpu.VMEM((n, LANES), f32),
        pltpu.VMEM((t, LANES), f32),
        pltpu.VMEM((n, LANES), f32),
        pltpu.VMEM((n, phases * 32), f32),
    ]
    block = jax.ShapeDtypeStruct((devices // 4, LANES + 8, LANES), f32)
    return pl.pallas_call(
        lambda *refs: early_kernel(*refs, phases=phases, devices=devices),
        out_shape=(block, block, jax.ShapeDtypeStruct(slide_shape(m, phases), bf16)),
        in_specs=[IN_VMEM] * (len(pieces) + 6),
        out_specs=(IN_VMEM,) * 3,
        scratch_shapes=shapes,
        compiler_params=grant(shapes),
        cost_estimate=pl.CostEstimate(flops=2**32, bytes_accessed=2**24, transcendentals=0),
        name="correlate_early",
    )(*pieces, w, norm, *energy, *rest)


def correlate_rest(slide, w, rest_acc, m, phases, devices):
    shapes = [pltpu.VMEM((m + rest_acc.shape[0], phases * 32), f32)]
    block = jax.ShapeDtypeStruct((devices // 4, LANES, LANES), f32)
    return pl.pallas_call(
        lambda *refs: rest_kernel(*refs, phases=phases, devices=devices),
        out_shape=(block, block),
        in_specs=[IN_VMEM] * 3,
        out_specs=(IN_VMEM, IN_VMEM),
        scratch_shapes=shapes,
        compiler_params=grant(shapes),
        cost_estimate=pl.CostEstimate(flops=2**33, bytes_accessed=2**24, transcendentals=0),
        name="correlate_rest",
    )(slide, w, rest_acc)


def cut(block, phases):
    per = L // phases
    half = per // 2
    starts = range(0, LANES, per)
    return (
        jnp.concatenate([block[at : at + half] for at in starts], axis=0),
        jnp.concatenate([block[at + half : at + per] for at in starts], axis=0),
    )


def halves_kernel(kept_ref, got_ref, mine_ref, other_ref, *, phases):
    first = lax.axis_index("win") % 2 == 0
    block = kept_ref[0] + got_ref[0]
    lower, upper = cut(block, phases)
    rows = LANES // 2
    mine_ref[0:rows] = jnp.where(first, lower, upper)
    other_ref[0:rows] = jnp.where(first, upper, lower)
    if block.shape[0] > LANES:
        mine_ref[rows:] = block[LANES:]
        other_ref[rows:] = block[LANES:]


def halves(kept, got, phases):
    half = jax.ShapeDtypeStruct((kept.shape[1] - LANES // 2, LANES), f32)
    return pl.pallas_call(
        lambda *refs: halves_kernel(*refs, phases=phases),
        out_shape=(half, half),
        in_specs=[IN_VMEM, IN_VMEM],
        out_specs=(IN_VMEM, IN_VMEM),
        compiler_params=SMALL,
        cost_estimate=pl.CostEstimate(flops=2**32, bytes_accessed=2**20, transcendentals=0),
        name="halves",
    )(kept, got)


def woven(straight, mine, got):
    groups = LANES // 2
    low = iota(mine.shape, 1) < groups
    zero, one = jnp.where(straight, mine, got), jnp.where(straight, got, mine)
    return jnp.where(low, zero, pltpu.roll(one, groups, 1)), jnp.where(low, pltpu.roll(zero, groups, 1), one)


def scale_kernel(mine_ref, got_ref, even_ref, odd_ref, mine_scale, got_scale, *, phases, devices):
    groups = LANES // 2
    per = L // phases
    half = per // 2
    tiles = phases // 4
    me = lax.axis_index("win")
    first = me % 2 == 0
    straight = panel_of(me, devices) == 0
    place = iota((LANES, LANES), 0)
    wanted = (place // (2 * phases)) * phases + place % (2 * phases) - phases
    gather = (
        ((place % (2 * phases) >= phases) & (iota((LANES, LANES), 1) % groups == wanted)).astype(f32).astype(bf16)
    )
    low = iota((half, LANES), 1) < groups
    sides = []
    for ref in (mine_ref, got_ref):
        extra = ref[groups:]
        norm = math.sqrt(CT * L) * lax.rsqrt(pick(extra, gather))[:1]
        scale = lax.rsqrt(extra + epsilon)
        scales = []
        for tile in range(2 * tiles):
            columns = []
            for phase in (2 * tile, 2 * tile + 1):
                if half >= 8:
                    count = half // 8
                    pieces = [scale[:, 2 * phases * k + phase :][:, :1] for k in range(2 * count)]
                    columns.append(
                        jnp.concatenate(
                            [jnp.where(first, pieces[k], pieces[k + count]) for k in range(count)], axis=0
                        )
                    )
                else:
                    columns.append(
                        jnp.where(first, scale[:half, phase : phase + 1], scale[half : 2 * half, phase : phase + 1])
                    )
            scales.append(jnp.where(low, columns[0], columns[1]) * norm)
        sides.append(scales)
    for tile in range(tiles):
        rows = slice(tile * half, (tile + 1) * half)
        mine_scale[rows] = sides[0][tiles + tile]
        got_scale[rows] = sides[1][tiles + tile]
        even_ref[rows], odd_ref[rows] = woven(
            straight, mine_ref[rows] * sides[0][tile], got_ref[rows] * sides[1][tile]
        )


def scaled(mine, got, phases, devices):
    half = jax.ShapeDtypeStruct((LANES // 2, LANES), f32)
    return pl.pallas_call(
        lambda *refs: scale_kernel(*refs, phases=phases, devices=devices),
        out_shape=(half,) * 4,
        in_specs=[IN_VMEM, IN_VMEM],
        out_specs=(IN_VMEM,) * 4,
        compiler_params=SMALL,
        cost_estimate=pl.CostEstimate(flops=2**32, bytes_accessed=2**18, transcendentals=0),
        name="scale",
    )(mine, got)


def finish_kernel(even_ref, odd_ref, mine_scale, got_scale, mine_ref, got_ref, out_ref, *, phases, devices):
    half = L // phases // 2
    tiles = phases // 4
    straight = panel_of(lax.axis_index("win"), devices) == 0
    mine = mine_ref[...] * mine_scale[...]
    got = got_ref[...] * got_scale[...]
    even, odd = woven(straight, mine, got)
    for tile in range(tiles):
        rows = slice(tile * half, (tile + 1) * half)
        for phase, value in enumerate((even_ref[rows], odd_ref[rows])):
            out_ref[pl.ds(2 * tile + phase, half, stride=phases), :] = value
        for phase, value in enumerate((even[rows], odd[rows])):
            out_ref[pl.ds(2 * (tiles + tile) + phase, half, stride=phases), :] = value


def finish(first, second, phases, devices):
    return pl.pallas_call(
        lambda *refs: finish_kernel(*refs, phases=phases, devices=devices),
        out_shape=jax.ShapeDtypeStruct((L // 2, LANES), f32),
        in_specs=[IN_VMEM] * 6,
        out_specs=IN_VMEM,
        compiler_params=SMALL,
        cost_estimate=pl.CostEstimate(flops=2**18, bytes_accessed=2**18, transcendentals=0),
        name="finish",
    )(*first, *second)


def masks_kernel(start_hbm, routed_ref, start_ref, sem, *, devices):
    copy = pltpu.make_async_copy(start_hbm, start_ref, sem)
    copy.start()
    held = routed_ref.shape[1]
    me = lax.axis_index("win")
    mine = panel_of(me, devices)
    per_chip = 2 * CT // devices
    row = iota((CT, held), 0)
    panels = (1 - mine, mine)
    channels = []
    for panel in panels:
        target = jnp.bitwise_xor(target_of(row // per_chip, panel, devices), me // 2)
        core = jnp.bitwise_xor(panel, panel_of(2 * target, devices))
        channel = target * per_chip + (row % per_chip + per_chip // 2 * core) % per_chip
        channels.append(channel - me * held - iota((CT, held), 1))
    copy.wait()
    for i, panel in enumerate(panels):
        routed_ref[i * CT : (i + 1) * CT] = (channels[i] + start_ref[panel] == 0).astype(f32).astype(bf16)


def masks(panel_start, held, devices):
    return pl.pallas_call(
        lambda *refs: masks_kernel(*refs, devices=devices),
        out_shape=jax.ShapeDtypeStruct((2 * CT, held), bf16),
        in_specs=[pl.BlockSpec(memory_space=pltpu.HBM)],
        out_specs=IN_VMEM,
        scratch_shapes=[pltpu.SMEM(panel_start.shape, jnp.int32), pltpu.SemaphoreType.DMA],
        compiler_params=SMALL,
        cost_estimate=pl.CostEstimate(flops=2**31, bytes_accessed=2**16, transcendentals=0),
        name="masks",
    )(panel_start)


def select_kernel(records_ref, routed_ref, *refs, begin):
    away_ref, home_ref = refs[-2:]
    both = dot(routed_ref[...], records_ref[:, begin : begin + away_ref.shape[1]]).astype(bf16)
    away_ref[...] = both[:CT]
    home_ref[...] = both[CT:]


def selected(records, routed, begin, end, *before):
    out = jax.ShapeDtypeStruct((CT, end - begin), bf16)
    return pl.pallas_call(
        lambda *refs: select_kernel(*refs, begin=begin),
        out_shape=(out, out),
        in_specs=[IN_VMEM, IN_VMEM] + [pl.BlockSpec(memory_space=pl.ANY)] * len(before),
        out_specs=(IN_VMEM, IN_VMEM),
        compiler_params=pltpu.CompilerParams(vmem_limit_bytes=SPARE),
        cost_estimate=pl.CostEstimate(flops=2**27, bytes_accessed=2**21, transcendentals=0),
        name="select",
    )(records, routed, *before)


def add_kernel(kept_ref, got_ref, *refs):
    keep_ref, send_ref = refs[-2:]
    half = keep_ref.shape[0]
    keep_ref[...] = kept_ref[:half] + got_ref[:half]
    send_ref[...] = kept_ref[half:] + got_ref[half:]


def added(kept, got, *before):
    half = kept.shape[0] // 2
    if kept.dtype == bf16 and half % 16:
        whole = kept + got
        return whole[:half], whole[half:]
    part = jax.ShapeDtypeStruct((half, *kept.shape[1:]), kept.dtype)
    return pl.pallas_call(
        add_kernel,
        out_shape=(part, part),
        in_specs=[IN_VMEM, IN_VMEM] + [pl.BlockSpec(memory_space=pl.ANY)] * len(before),
        out_specs=(IN_VMEM, IN_VMEM),
        compiler_params=SMALL,
        cost_estimate=pl.CostEstimate(flops=2**32, bytes_accessed=2**20, transcendentals=0),
        name="add",
    )(kept, got, *before)


def local(records, templates, panel_start):
    devices = lax.axis_size("win")
    panel = panel_of(lax.axis_index("win"), devices)
    phases = devices // 2
    pairs = (L // phases + 2) // 2
    orders = bits_of(devices)
    steps = len(orders[0])

    def sibling(value):
        return lax.ppermute(value, "win", [(d, d ^ 1) for d in range(devices)])

    def exchange(value, step):
        return lax.ppermute(value, "win", [(d, d ^ 1 ^ orders[panel_of(d, devices)][step]) for d in range(devices)])

    def scattered(keep, send, until, before=()):
        for step in range(until - 1):
            keep, send = added(keep, exchange(send, step), *(before if step == 0 else ()))
        return keep, exchange(send, until - 1)

    half = records.shape[1] // 2
    routed = masks(panel_start, records.shape[0], devices)
    away_late, home_late = selected(records, routed, half, 2 * half)
    got_late = sibling(away_late)
    away_early, home_early = selected(records, routed, 0, half, away_late)
    got_early = sibling(away_early)

    templates = templates.reshape(templates.shape[0], -1, L)
    other = sibling(given(templates, away_early, devices))
    late = added(home_late, got_late)
    early = added(home_early, got_early, late[0])
    w, norm = shifted(templates, other, phases, pairs, early[0])
    held = late, early
    for step in range(steps - 1):
        if step == 0:
            late_energy, squares = energy_of(held[0], [], norm, phases)
        late = added(late[0], exchange(late[1], step), *([late_energy] if step == 0 else []))
        if step == 0:
            early_energy, _ = energy_of(held[1], [squares], late[0], phases)
        early = added(early[0], exchange(early[1], step), *([early_energy] if step == 0 else []))
    late, early = [(keep, exchange(send, steps - 1)) for keep, send in (late, early)]
    rest_rows, rest_acc = correlate_late(late, w, phases)
    energy = early_energy, late_energy
    send_a, keep_a, slide = correlate_early(early, w, norm, energy, (rest_rows, rest_acc), phases, devices)
    send_b, keep_b = correlate_rest(slide, w, rest_acc, half // phases, phases, devices)

    mine, other = halves(*scattered(keep_a, send_a, steps, [send_b]), phases)
    first = scaled(mine, sibling(other), phases, devices)
    mine, other = halves(*scattered(keep_b, send_b, steps), phases)
    return finish(first, (mine, sibling(other)), phases, devices)


def solution(mesh):
    placed = (P("win", "parts"), P(None, None, "win", None), P("parts"))
    return jax.shard_map(
        local, mesh=mesh, in_specs=placed, out_specs=P(("parts", "win"), None), check_vma=False
    )
```
